256 devices in a mesh: row: 32 (over z, y_hi, core), col: 8 (over y_lo, x).
Axes of the slice: x: 4, y: 4 (y_hi: 2, y_lo: 2; y = y_hi * 2 + y_lo), z: 8, core: 2. Of those that a mesh axis runs over, the one named last changes fastest.
Arguments:
- density: bfloat16 [8192, 8192], P('row', 'col'), as said below
- pattern: int32 [32, 32], replicated, may hold values from 0 to 1, as said below
- tile_perm: int32 [32], replicated, may hold values from 0 to 31, each once
Outputs:
- square: float32 [8192, 8192], P('row', 'col')
- cubed: float32 [8192, 8192], P('row', 'col')
The draws below stay inside these ranges and needn't reach their ends.
Inputs may be any that keep to these rules, and one draw needn't show every extreme that they name: `pattern`: zero below the diagonal, one on the diagonal, ones above it near the diagonal and scattered further away; every tile row of sym_pattern holds at most 13 ones, and some tile row holds exactly 13. density is exactly symmetric.
All inputs are finite; a program needn't handle non-finite values.
Results may differ from the reference program's by a relative error of at most 0.0021.
Values may be sent and summed in bfloat16 or wider, within the bound.
No kernel may reach another device: no remote copies, remote signals or barrier semaphores. Data moves between devices by JAX's collectives and lax.ppermute only.
A program may use at most 64 MiB of HBM per device.

```python
import jax
import jax.numpy as jnp

TILE = 256
NTILES = 32
ORDER = 8192


def draw_pattern(key, part):
    key = jax.random.fold_in(key, 1)
    band_width = max(NTILES // 16, 1)
    far_count = NTILES // 8
    candidates = NTILES // 2 - band_width - 1
    offsets = band_width + 1 + jax.random.permutation(jax.random.fold_in(key, 7), candidates)[:far_count]
    tile_index = jnp.arange(NTILES, dtype=jnp.int32)
    above = tile_index[None, :] - tile_index[:, None]
    is_far = jnp.any(above[:, :, None] == offsets[None, None, :].astype(jnp.int32), axis=2)
    coins = jax.random.randint(key, (NTILES, NTILES), 0, 2)
    centre = NTILES // 2
    forced = (tile_index[:, None] == centre) | (tile_index[None, :] == centre)
    near_band = (above >= 0) & (above <= band_width)
    keep_tile = near_band | is_far & ((coins == 0) | forced)
    return keep_tile.astype(jnp.int32)


def draw_density(key, part):
    key = jax.random.fold_in(key, 2)
    values = jax.random.normal(key, (ORDER, ORDER), jnp.float32)
    symmetric = (values + values.T) * 0.5 ** 0.5
    return (symmetric * (ORDER / 2.0) ** (-0.25)).astype(jnp.bfloat16)


def setup_inputs(seed: int = 0) -> dict:
    keys = jax.random.split(jax.random.key(seed), 4)
    density = draw_density(jax.random.fold_in(keys[3], 71), 0)
    pattern = draw_pattern(jax.random.fold_in(keys[3], 71), 0)
    tile_perm = jax.random.permutation(keys[2], NTILES).astype(jnp.int32)
    return dict(density=density, pattern=pattern, tile_perm=tile_perm)


def build_mask(pattern, tile_perm):
    count = pattern.shape[0]
    tile_index = jnp.arange(count, dtype=jnp.int32)
    symmetric = jnp.where(tile_index[:, None] <= tile_index[None, :], pattern, pattern.T)
    return symmetric[tile_perm][:, tile_perm]


def apply_mask(matrix, tile_mask):
    count = matrix.shape[0] // TILE
    blocks = matrix.reshape(count, TILE, count, TILE) * tile_mask[:, None, :, None].astype(matrix.dtype)
    return blocks.reshape(matrix.shape)


def reference(density, pattern, tile_perm):
    tile_mask = build_mask(pattern, tile_perm)
    matrix = apply_mask(density, tile_mask)
    square = apply_mask(jnp.dot(matrix, matrix, preferred_element_type=jnp.float32), tile_mask)
    square_half = square.astype(jnp.bfloat16)
    scale_factor = (ORDER / 2.0) ** -0.25
    cubed = apply_mask(jnp.dot(square_half, matrix, preferred_element_type=jnp.float32), tile_mask) * scale_factor
    return square, cubed
```

```python
import jax
import jax.numpy as jnp
from jax import lax
from jax.experimental import pallas as pl
from jax.experimental.pallas import tpu as pltpu
from jax.sharding import PartitionSpec as P

TILE = 256
SLOTS = 13
BOTH = ("row", "col")
VMEM_LIMIT = 48 * 1024 * 1024


def in_vmem(count):
    return [pl.BlockSpec(memory_space=pltpu.VMEM)] * count


def in_smem(count):
    return [pl.BlockSpec(memory_space=pltpu.SMEM)] * count


def params():
    return pltpu.CompilerParams(vmem_limit_bytes=VMEM_LIMIT)


SIZES = dict(z=8, y_hi=2, core=2, y_lo=2, x=4)


def shift_pairs(**steps):
    pairs = []
    for source in range(256):
        at, rest = {}, source
        for name in ("x", "y_lo", "core", "y_hi", "z"):
            at[name] = rest % SIZES[name]
            rest //= SIZES[name]
        for name, step in steps.items():
            at[name] = (at[name] + step) % SIZES[name]
        target = 0
        for name in ("z", "y_hi", "core", "y_lo", "x"):
            target = target * SIZES[name] + at[name]
        pairs.append((source, target))
    return pairs


def move(block, **steps):
    return lax.ppermute(block, BOTH, shift_pairs(**steps))


def spread_col(block):
    moved = []
    for y_step in (0, 1):
        for x_step in (1, 3, 2, 0):
            if y_step or x_step:
                moved.append((move(block, y_lo=y_step, x=x_step), y_step, x_step))
    return moved


COL_STEPS = [(y, x) for y in (0, 1) for x in (1, 3, 2, 0) if y or x]


def col_source(col, y_step, x_step):
    y_lo, x = col // 4, col % 4
    return ((y_lo + 2 - y_step) % 2) * 4 + (x + 4 - x_step) % 4


def table_kernel(pattern_ref, perm_ref, table_ref):
    count = pattern_ref.shape[0]
    first = lax.broadcasted_iota(jnp.int32, (count, count), 0)
    second = lax.broadcasted_iota(jnp.int32, (count, count), 1)
    pattern = pattern_ref[...].astype(jnp.float32)
    one_hot = (perm_ref[...] == second).astype(jnp.float32)
    upper = jnp.where(first <= second, pattern, 0.0)
    strict = jnp.where(first < second, pattern, 0.0)

    def dot(a, b, b_dim):
        return lax.dot_general(
            a, b, (((1,), (b_dim,)), ((), ())), preferred_element_type=jnp.float32
        )

    mask = dot(dot(one_hot, upper, 0) + dot(one_hot, strict, 1), one_hot, 1)
    rank = dot(mask, (first < second).astype(jnp.float32), 0).astype(jnp.int32)
    slot = jnp.where(mask > 0.5, rank, -1)
    table_ref[:, :count] = slot
    lane = lax.broadcasted_iota(jnp.int32, (count, count), 1)
    order = jnp.zeros((count, count), jnp.int32)
    for place in range(SLOTS):
        tile = jnp.sum(jnp.where(slot == place, second, 0), axis=1, keepdims=True)
        order = jnp.where(lane == place, tile, order)
    ones = jnp.sum((slot >= 0).astype(jnp.int32), axis=1, keepdims=True)
    order = jnp.where(lane == SLOTS, ones, order)
    table_ref[:, count:] = order


def tables(pattern, tile_perm):
    count = pattern.shape[0]
    return pl.pallas_call(
        table_kernel,
        out_shape=jax.ShapeDtypeStruct((count, 2 * count), jnp.int32),
        in_specs=in_vmem(2),
        out_specs=pl.BlockSpec(memory_space=pltpu.VMEM),
    )(pattern, tile_perm[:, None])


def pack_kernel(table_ref, strips_ref, packed_ref):
    count = table_ref.shape[0]
    row = lax.axis_index("row")
    per_col = strips_ref.shape[2] // TILE
    ones = table_ref[row, count + SLOTS]
    for place in range(SLOTS):
        tile = table_ref[row, count + place]
        start = pl.multiple_of((tile % per_col) * TILE, TILE)
        block = strips_ref[tile // per_col, :, pl.ds(start, TILE)]
        packed_ref[:, place * TILE : (place + 1) * TILE] = jnp.where(
            place < ones, block, jnp.zeros_like(block)
        )


def pack(table, strips):
    depth = strips.shape[1]
    return pl.pallas_call(
        pack_kernel,
        out_shape=jax.ShapeDtypeStruct((depth, SLOTS * TILE), strips.dtype),
        in_specs=in_smem(1) + in_vmem(1),
        out_specs=pl.BlockSpec(memory_space=pltpu.VMEM),
        compiler_params=params(),
    )(table, strips)


def square_kernel(table_ref, *refs, places):
    pieces, blocks = refs[:8], refs[8:40]
    half_ref, low_ref, factor_ref, band = refs[40:]
    count = table_ref.shape[0]
    row, col = lax.axis_index("row"), lax.axis_index("col")
    z, y_hi, core = row // 4, (row // 2) % 2, row % 2
    depth = pieces[0].shape[0]
    for piece, (y_step, x_step) in zip(pieces, [(0, 0)] + COL_STEPS):
        strip = col_source(col, y_step, x_step)
        band[pl.ds(pl.multiple_of(strip * depth, depth), depth), :] = piece[...]
    factor_ref[...] = jnp.zeros_like(factor_ref)
    ones = table_ref[row, count + SLOTS]
    for block, (z_step, y_step, core_step) in zip(blocks, places):
        other = ((z + 8 - z_step) % 8) * 4 + ((y_hi + y_step) % 2) * 2 + (core + core_step) % 2
        place = table_ref[row, other]

        @pl.when(place >= 0)
        def _():
            start = pl.multiple_of(place * depth, depth)

            def copy(inner, _):
                slot = table_ref[other, table_ref[row, count + inner]]

                @pl.when(slot >= 0)
                def _():
                    factor_ref[
                        pl.ds(start, depth), pl.ds(pl.multiple_of(inner * TILE, TILE), TILE)
                    ] = block[:, pl.ds(pl.multiple_of(slot * TILE, TILE), TILE)]

                return 0

            lax.fori_loop(0, ones, copy, 0)

    square = lax.dot_general(
        factor_ref[...], band[...], (((1,), (1,)), ((), ())), preferred_element_type=jnp.float32
    )
    half = square.astype(jnp.bfloat16)
    half_ref[...] = half
    low_ref[...] = (square - half.astype(jnp.float32)).astype(jnp.bfloat16)


def square_strips(table, pieces, blocks, places):
    depth, width = pieces[0].shape
    strip = jax.ShapeDtypeStruct((SLOTS * depth, TILE), jnp.bfloat16)
    return pl.pallas_call(
        lambda *refs: square_kernel(*refs, places=places),
        out_shape=(strip, strip, jax.ShapeDtypeStruct((SLOTS * depth, width), jnp.bfloat16)),
        in_specs=in_smem(1) + in_vmem(40),
        out_specs=[pl.BlockSpec(memory_space=pltpu.VMEM)] * 3,
        scratch_shapes=[pltpu.VMEM((TILE, width), jnp.bfloat16)],
        compiler_params=params(),
    )(table, *pieces, *blocks)


def cube_kernel(table_ref, factor_ref, low_ref, *refs, scale):
    pieces, (sent_ref, whole, total) = refs[:8], refs[8:]
    count = table_ref.shape[0]
    row, col = lax.axis_index("row"), lax.axis_index("col")
    depth = factor_ref.shape[0] // SLOTS
    for piece, (y_step, x_step) in zip(pieces, [(0, 0)] + COL_STEPS):
        strip = col_source(col, y_step, x_step)
        for place in range(SLOTS):
            start = pl.multiple_of(place * TILE + strip * depth, depth)
            whole[pl.ds(start, depth), :] = piece[place * depth : (place + 1) * depth, :]
    total[...] = scale * jnp.dot(
        factor_ref[...], whole[...], preferred_element_type=jnp.float32
    )
    per_col = sent_ref.shape[1] // 3
    for tile in range(count):
        place = table_ref[row, tile]
        start = pl.multiple_of(jnp.maximum(place, 0) * depth, depth)
        cube = jnp.where(place >= 0, total[pl.ds(start, depth), :], 0.0)
        low = low_ref[pl.ds(start, depth), :]
        high = cube.astype(jnp.bfloat16)
        to, spot = tile // per_col, tile % per_col
        sent_ref[to, spot] = high
        sent_ref[to, per_col + spot] = (cube - high.astype(jnp.float32)).astype(jnp.bfloat16)
        sent_ref[to, 2 * per_col + spot] = jnp.where(place >= 0, low, jnp.zeros_like(low))


def cube_strips(table, factor, low, pieces, per_col, cols, scale):
    depth = factor.shape[0] // SLOTS
    return pl.pallas_call(
        lambda *refs: cube_kernel(*refs, scale=scale),
        out_shape=jax.ShapeDtypeStruct((cols, 3 * per_col, depth, TILE), jnp.bfloat16),
        in_specs=in_smem(1) + in_vmem(10),
        out_specs=pl.BlockSpec(memory_space=pltpu.VMEM),
        scratch_shapes=[
            pltpu.VMEM((SLOTS * TILE, TILE), jnp.bfloat16),
            pltpu.VMEM((SLOTS * depth, TILE), jnp.float32),
        ],
        compiler_params=params(),
    )(table, factor, low, *pieces)


def home_kernel(table_ref, got_ref, *refs):
    pieces, (square_ref, cubed_ref, held) = refs[:8], refs[8:]
    row, col = lax.axis_index("row"), lax.axis_index("col")
    cols, _, depth, _ = got_ref.shape
    per_col = square_ref.shape[1] // TILE
    for spot in range(per_col):
        columns = slice(spot * TILE, (spot + 1) * TILE)
        for strip in range(cols):
            held[strip * depth : (strip + 1) * depth, :] = got_ref[strip, spot].astype(
                jnp.float32
            ) + got_ref[strip, per_col + spot].astype(jnp.float32)
        cubed_ref[:, columns] = held[...].T
        place = table_ref[row, col * per_col + spot]
        start = pl.multiple_of(jnp.maximum(place, 0) * depth, depth)
        for piece, (y_step, x_step) in zip(pieces, [(0, 0)] + COL_STEPS):
            strip = col_source(col, y_step, x_step)
            high = piece[pl.ds(start, depth), :].astype(jnp.float32)
            low = got_ref[strip, 2 * per_col + spot].astype(jnp.float32)
            held[pl.ds(pl.multiple_of(strip * depth, depth), depth), :] = jnp.where(
                place >= 0, high + low, 0.0
            )
        square_ref[:, columns] = held[...].T


def home(table, got, pieces, shape):
    out = jax.ShapeDtypeStruct(shape, jnp.float32)
    return pl.pallas_call(
        home_kernel,
        out_shape=(out, out),
        in_specs=in_smem(1) + in_vmem(9),
        out_specs=[pl.BlockSpec(memory_space=pltpu.VMEM)] * 2,
        scratch_shapes=[pltpu.VMEM((TILE, TILE), jnp.float32)],
        compiler_params=params(),
    )(table, got, *pieces)


def local(density, pattern, tile_perm):
    rows, columns = density.shape
    cols = lax.axis_size("col")
    per_col = columns // TILE
    table = tables(pattern, tile_perm)
    strips = lax.all_to_all(
        density.reshape(cols, rows // cols, columns), "col", split_axis=0, concat_axis=0
    )
    packed = pack(table, strips)
    pieces = [packed] + [block for block, _, _ in spread_col(packed)]
    blocks, places = [packed], [(0, 0, 0)]
    across = move(packed, y_hi=1)
    up, down = packed, packed
    up_across, down_across = across, across
    blocks.append(across)
    places.append((0, 1, 0))
    for step in (1, 2, 3, 4):
        up = move(up, z=1)
        blocks.append(up)
        places.append((step, 0, 0))
        down_across = move(down_across, z=-1)
        blocks.append(down_across)
        places.append((-step, 1, 0))
        if step < 4:
            down = move(down, z=-1)
            blocks.append(down)
            places.append((-step, 0, 0))
            up_across = move(up_across, z=1)
            blocks.append(up_across)
            places.append((step, 1, 0))
    swapped = [move(block, core=1) for block in blocks]
    places = places + [(z, y, 1) for z, y, _ in places]
    half, low, factor = square_strips(table, pieces, blocks + swapped, places)
    pieces = [half] + [block for block, _, _ in spread_col(half)]
    scale = (rows * lax.axis_size("row") / 2.0) ** (-0.25)
    sent = cube_strips(table, factor, low, pieces, per_col, cols, scale)
    got = lax.all_to_all(sent, "col", split_axis=0, concat_axis=0)
    return home(table, got, pieces, (rows, columns))


def solution(mesh):
    return jax.shard_map(
        local,
        mesh=mesh,
        in_specs=(P("row", "col"), P(), P()),
        out_specs=(P("row", "col"), P("row", "col")),
        check_vma=False,
    )
```

```python
import functools

import jax
import jax.numpy as jnp
from jax import lax
from jax.experimental import pallas as pl
from jax.experimental.pallas import tpu as pltpu
from jax.sharding import PartitionSpec as P

TILE = 256
SLOTS = 13
BOTH = ("row", "col")
MIB = 1024 * 1024
VMEM = pl.BlockSpec(memory_space=pltpu.VMEM)
SMEM = pl.BlockSpec(memory_space=pltpu.SMEM)

Z, Y_HI, CORE, COL = 8, 2, 2, 8


def device(z, y_hi, core, col):
    return ((z % Z * Y_HI + y_hi % Y_HI) * CORE + core % CORE) * COL + col


def pairs(move):
    places = [
        (z, y_hi, core, col)
        for z in range(Z)
        for y_hi in range(Y_HI)
        for core in range(CORE)
        for col in range(COL)
    ]
    return [(device(*place), device(*move(*place))) for place in places]


def move(block, place):
    return lax.ppermute(block, BOTH, pairs(place))


def to_other_core(block):
    return move(block, lambda z, y, core, col: (z, y, core + 1, col))


def to_other_y(block):
    return move(block, lambda z, y, core, col: (z, y + 1, core, col))


def along_z(block, steps=1):
    return move(block, lambda z, y, core, col: (z + steps * (1 - 2 * core), y, core, col))


def call(kernel, out_shape, operands, tables=1, loose=0, limit=16, **options):
    held = len(operands) - tables - loose
    return pl.pallas_call(
        kernel,
        out_shape=out_shape,
        in_specs=[SMEM] * tables + [VMEM] * held + [pl.BlockSpec(memory_space=pltpu.HBM)] * loose,
        out_specs=jax.tree.map(lambda _: VMEM, out_shape),
        compiler_params=pltpu.CompilerParams(vmem_limit_bytes=limit * MIB),
        **options,
    )(*operands)


def table_kernel(pattern_ref, perm_ref, table_ref):
    count = pattern_ref.shape[0]
    first = lax.broadcasted_iota(jnp.int32, (count, count), 0)
    second = lax.broadcasted_iota(jnp.int32, (count, count), 1)
    pattern = pattern_ref[...].astype(jnp.float32)
    one_hot = (perm_ref[...] == second).astype(jnp.float32)
    upper = jnp.where(first <= second, pattern, 0.0)
    strict = jnp.where(first < second, pattern, 0.0)

    def dot(a, b, b_dim):
        return lax.dot_general(
            a, b, (((1,), (b_dim,)), ((), ())), preferred_element_type=jnp.float32
        )

    mask = dot(dot(one_hot, upper, 0) + dot(one_hot, strict, 1), one_hot, 1)
    rank = dot(mask, (first < second).astype(jnp.float32), 0).astype(jnp.int32)
    slot = jnp.where(mask > 0.5, rank, -1)
    order = jnp.zeros((count, count), jnp.int32)
    for place in range(SLOTS):
        tile = jnp.sum(jnp.where(slot == place, second, 0), axis=1, keepdims=True)
        order = jnp.where(second == place, tile, order)
    ones = jnp.sum((slot >= 0).astype(jnp.int32), axis=1, keepdims=True)
    order = jnp.where(second == SLOTS, ones, order)
    table_ref[:, :count] = slot
    table_ref[:, count:] = order


def tables(pattern, tile_perm):
    count = pattern.shape[0]
    shape = jax.ShapeDtypeStruct((count, 2 * count), jnp.int32)
    return call(table_kernel, shape, (pattern, tile_perm[:, None]), tables=0)


def place_of(row):
    return row // 4, (row // 2) % 2, row % 2


def pack_kernel(table_ref, strips_ref, packed_ref, spread_ref):
    count = table_ref.shape[0]
    row = lax.axis_index("row")
    per_col = strips_ref.shape[2] // TILE
    ones = table_ref[row, count + SLOTS]
    for place in range(SLOTS):
        tile = table_ref[row, count + place]
        start = pl.multiple_of((tile % per_col) * TILE, TILE)
        block = strips_ref[tile // per_col, :, pl.ds(start, TILE)]
        block = jnp.where(place < ones, block, jnp.zeros_like(block))
        columns = slice(place * TILE, (place + 1) * TILE)
        packed_ref[:, columns] = block
        for col in range(COL):
            spread_ref[col, :, columns] = block


def pack(table, strips):
    _, depth, _ = strips.shape
    width = SLOTS * TILE
    shapes = (
        jax.ShapeDtypeStruct((depth, width), strips.dtype),
        jax.ShapeDtypeStruct((COL, depth, width), strips.dtype),
    )
    return call(pack_kernel, shapes, (table, strips), limit=8)


def fill(table_ref, factor_ref, blocks, places, strips, arrived, fresh):
    count = table_ref.shape[0]
    depth = strips.shape[1]
    row = lax.axis_index("row")
    z, y_hi, core = place_of(row)
    ones = table_ref[row, count + SLOTS]
    jobs = []
    for block, (step, y_flip, core_flip) in zip(blocks, places):
        passed_by = core ^ core_flip
        z_of = (z + Z + step * (2 * passed_by - 1)) % Z
        for half in range(block.shape[0] // depth):
            other = (z_of * Y_HI + (y_hi ^ y_flip)) * CORE + (passed_by ^ half)
            index = len(jobs)
            fetch = pltpu.make_async_copy(
                block.at[pl.ds(half * depth, depth), :], strips.at[index], arrived.at[index]
            )
            jobs.append((table_ref[row, other], other, fetch))
    for place, _, fetch in jobs:
        pl.when(place >= 0)(fetch.start)
    if fresh:
        factor_ref[...] = jnp.zeros_like(factor_ref)
    for index, (place, other, fetch) in enumerate(jobs):

        @pl.when(place >= 0)
        def _(index=index, place=place, other=other, fetch=fetch):
            fetch.wait()
            start = pl.multiple_of(place * depth, depth)

            def copy(inner, _):
                slot = table_ref[other, table_ref[row, count + inner]]

                @pl.when(slot >= 0)
                def _():
                    factor_ref[
                        pl.ds(start, depth), pl.ds(pl.multiple_of(inner * TILE, TILE), TILE)
                    ] = strips[index, :, pl.ds(pl.multiple_of(slot * TILE, TILE), TILE)]

                return 0

            lax.fori_loop(0, ones, copy, 0)


def fill_scratch(blocks, depth):
    jobs = sum(block.shape[0] // depth for block in blocks)
    return [
        pltpu.VMEM((jobs, depth, blocks[0].shape[1]), blocks[0].dtype),
        pltpu.SemaphoreType.DMA((jobs,)),
    ]


def first_kernel(table_ref, *refs, places):
    fill(table_ref, refs[-3], refs[:-3], places, refs[-2], refs[-1], True)


def next_kernel(table_ref, _, *refs, places):
    fill(table_ref, refs[-3], refs[:-3], places, refs[-2], refs[-1], False)


def grow(table, factor, arrived, depth):
    blocks, places = zip(*arrived)
    width = blocks[0].shape[1]
    shape = jax.ShapeDtypeStruct((SLOTS * depth, width), blocks[0].dtype)
    options = dict(loose=len(blocks), limit=12, scratch_shapes=fill_scratch(blocks, depth))
    if factor is None:
        kernel = functools.partial(first_kernel, places=places)
        return call(kernel, shape, (table, *blocks), **options)
    kernel = functools.partial(next_kernel, places=places)
    return call(kernel, shape, (table, factor, *blocks), input_output_aliases={1: 0}, **options)


def square_kernel(table_ref, _, band_ref, *refs, places):
    blocks, (spread_ref, square_ref, factor_ref, strips, arrived) = refs[:-5], refs[-5:]
    fill(table_ref, factor_ref, blocks, places, strips, arrived, False)
    band = band_ref[...].reshape(TILE, band_ref.shape[2])
    square = lax.dot_general(
        factor_ref[...], band, (((1,), (1,)), ((), ())), preferred_element_type=jnp.float32
    )
    square_ref[...] = square
    half = square.astype(jnp.bfloat16)
    for col in range(COL):
        spread_ref[col] = half


def square_strips(table, factor, band, arrived):
    blocks, places = zip(*arrived)
    rows = factor.shape[0]
    shapes = (
        jax.ShapeDtypeStruct((COL, rows, TILE), jnp.bfloat16),
        jax.ShapeDtypeStruct((rows, TILE), jnp.float32),
        jax.ShapeDtypeStruct(factor.shape, factor.dtype),
    )
    return call(
        functools.partial(square_kernel, places=places),
        shapes,
        (table, factor, band, *blocks),
        loose=len(blocks),
        input_output_aliases={1: 2},
        scratch_shapes=fill_scratch(blocks, band.shape[1]),
    )


def code(values, coded_ref, to, first):
    rows = values.shape[0]
    largest = jnp.max(jnp.abs(values), axis=0, keepdims=True)
    exponent = jnp.floor(jnp.log2(jnp.maximum(largest, 2.0**-100)))
    steps = jnp.round(values * jnp.exp2(14.0 - exponent))
    steps = jnp.clip(steps, -32767.0, 32767.0)
    coded_ref[to, first : first + rows, :] = steps.astype(jnp.int32).astype(jnp.int16)
    return jnp.broadcast_to(exponent, (8, values.shape[1]))


def cube_kernel(table_ref, factor_ref, square_ref, got_ref, coded_ref, whole, total, *, scale):
    count = table_ref.shape[0]
    row = lax.axis_index("row")
    cols, rows, _ = got_ref.shape
    depth = rows // SLOTS
    for strip in range(cols):
        for place in range(SLOTS):
            start = place * TILE + strip * depth
            whole[start : start + depth, :] = got_ref[
                strip, place * depth : (place + 1) * depth, :
            ]
    total[...] = scale * jnp.dot(
        factor_ref[...], whole[...], preferred_element_type=jnp.float32
    )
    per_col = count // cols
    for to in range(cols):
        marks = []
        for index, source in enumerate((total, square_ref)):
            values = []
            for spot in range(per_col):
                place = table_ref[row, to * per_col + spot]
                start = pl.multiple_of(jnp.maximum(place, 0) * depth, depth)
                values.append(jnp.where(place >= 0, source[pl.ds(start, depth), :], 0.0))
            values = jnp.concatenate(values, axis=0)
            marks.append(code(values, coded_ref, to, index * per_col * depth))
        marks = jnp.concatenate(marks, axis=0)
        coded_ref[to, 2 * per_col * depth :, :] = marks.astype(jnp.int32).astype(jnp.int16)


def cube_strips(table, factor, square, got, scale):
    cols, rows, _ = got.shape
    depth = rows // SLOTS
    per_col = table.shape[0] // cols
    shape = jax.ShapeDtypeStruct((cols, 2 * per_col * depth + 16, TILE), jnp.int16)
    return call(
        functools.partial(cube_kernel, scale=scale),
        shape,
        (table, factor, square, got),
        scratch_shapes=[
            pltpu.VMEM((SLOTS * TILE, TILE), jnp.bfloat16),
            pltpu.VMEM((rows, TILE), jnp.float32),
        ],
    )


def home_kernel(got_ref, square_ref, cubed_ref, held):
    cols, rows, _ = got_ref.shape
    per_col = square_ref.shape[1] // TILE
    depth = TILE // cols
    sizes = []
    for strip in range(cols):
        marks = got_ref[strip, rows - 16 :, :].astype(jnp.int32).astype(jnp.float32)
        sizes.append(jnp.exp2(marks - 14.0))
    for index, out_ref in enumerate((cubed_ref, square_ref)):
        for spot in range(per_col):
            for strip in range(cols):
                start = (index * per_col + spot) * depth
                steps = got_ref[strip, start : start + depth, :].astype(jnp.int32)
                size = sizes[strip][index * 8 : index * 8 + 1, :]
                held[strip * depth : (strip + 1) * depth, :] = steps.astype(jnp.float32) * size
            out_ref[:, spot * TILE : (spot + 1) * TILE] = held[...].T


def home(got, shape):
    out = jax.ShapeDtypeStruct(shape, jnp.float32)
    return call(
        home_kernel,
        (out, out),
        (got,),
        tables=0,
        scratch_shapes=[pltpu.VMEM((TILE, TILE), jnp.float32)],
    )


def local(density, pattern, tile_perm):
    rows, columns = density.shape
    depth = rows // COL
    table = tables(pattern, tile_perm)
    strips = lax.all_to_all(density.reshape(COL, depth, columns), "col", 0, 0)
    packed, spread = pack(table, strips)
    across = to_other_y(packed)
    near = [jnp.concatenate([packed, to_other_core(packed)], 0)]
    far = [jnp.concatenate([across, to_other_core(across)], 0)]

    def both(blocks, step, y_flip):
        return [
            (blocks[step], (step, y_flip, 0)),
            (to_other_core(blocks[step]), (step, y_flip, 1)),
        ]

    near.append(along_z(near[0]))
    far.append(along_z(far[0]))
    near[1], spread = lax.optimization_barrier((near[1], spread))
    band = lax.all_to_all(spread, "col", 0, 0)
    near.append(along_z(near[1]))
    far.append(along_z(far[1]))
    near.append(along_z(near[2]))
    far.append(along_z(far[2]))
    factor = grow(
        table, None, [(near[0], (0, 0, 0)), (far[0], (0, 1, 0))] + both(near, 1, 0), depth
    )
    near[3], factor = lax.optimization_barrier((near[3], factor))
    near.append(along_z(near[3][:depth]))
    factor = grow(table, factor, both(far, 1, 1) + both(near, 2, 0), depth)
    near[4], far[3], factor = lax.optimization_barrier((near[4], far[3], factor))
    far.append(along_z(far[3][:depth]))
    factor = grow(table, factor, both(far, 2, 1) + both(near, 3, 0), depth)
    spread, square, factor = square_strips(
        table, factor, band, both(far, 3, 1) + both(near, 4, 0) + both(far, 4, 1)
    )
    got = lax.all_to_all(spread, "col", 0, 0)
    scale = (rows * lax.axis_size("row") / 2.0) ** (-0.25)
    coded = cube_strips(table, factor, square, got, scale)
    return home(lax.all_to_all(coded, "col", 0, 0), (rows, columns))


def solution(mesh):
    return jax.shard_map(
        local,
        mesh=mesh,
        in_specs=(P("row", "col"), P(), P()),
        out_specs=(P("row", "col"), P("row", "col")),
        check_vma=False,
    )
```

```python
import functools

import jax
import jax.numpy as jnp
from jax import lax
from jax.experimental import pallas as pl
from jax.experimental.pallas import tpu as pltpu
from jax.sharding import PartitionSpec as P

TILE = 256
SLOTS = 13
BOTH = ("row", "col")
MIB = 1024 * 1024
VMEM = pl.BlockSpec(memory_space=pltpu.VMEM)
SMEM = pl.BlockSpec(memory_space=pltpu.SMEM)

Z, Y_HI, CORE, COL, X = 8, 2, 2, 8, 4


def device(z, y_hi, core, col):
    return ((z % Z * Y_HI + y_hi % Y_HI) * CORE + core % CORE) * COL + col


def pairs(move):
    places = [
        (z, y_hi, core, col)
        for z in range(Z)
        for y_hi in range(Y_HI)
        for core in range(CORE)
        for col in range(COL)
    ]
    return [(device(*place), device(*move(*place))) for place in places]


def move(block, place):
    return lax.ppermute(block, BOTH, pairs(place))


def to_other_core(block):
    return move(block, lambda z, y, core, col: (z, y, core + 1, col))


def to_other_y(block):
    return move(block, lambda z, y, core, col: (z, y + 1, core, col))


def to_other_y_lo(block):
    return move(block, lambda z, y, core, col: (z, y, core, (col + X) % COL))


def along_x(block):
    return move(
        block,
        lambda z, y, core, col: (z, y, core, col // X * X + (col + 1 - 2 * core) % X),
    )


def along_z(block, steps=1):
    return move(block, lambda z, y, core, col: (z + steps * (1 - 2 * core), y, core, col))


def call(kernel, out_shape, operands, tables=1, limit=16, **options):
    return pl.pallas_call(
        kernel,
        out_shape=out_shape,
        in_specs=[SMEM] * tables + [VMEM] * (len(operands) - tables),
        out_specs=jax.tree.map(lambda _: VMEM, out_shape),
        compiler_params=pltpu.CompilerParams(vmem_limit_bytes=limit * MIB),
        **options,
    )(*operands)


def table_kernel(pattern_ref, perm_ref, table_ref):
    count = pattern_ref.shape[0]
    first = lax.broadcasted_iota(jnp.int32, (count, count), 0)
    second = lax.broadcasted_iota(jnp.int32, (count, count), 1)
    pattern = pattern_ref[...].astype(jnp.float32)
    one_hot = (perm_ref[...] == second).astype(jnp.float32)
    upper = jnp.where(first <= second, pattern, 0.0)
    strict = jnp.where(first < second, pattern, 0.0)

    def dot(a, b, b_dim):
        return lax.dot_general(
            a, b, (((1,), (b_dim,)), ((), ())), preferred_element_type=jnp.float32
        )

    mask = dot(dot(one_hot, upper, 0) + dot(one_hot, strict, 1), one_hot, 1)
    rank = dot(mask, (first < second).astype(jnp.float32), 0).astype(jnp.int32)
    slot = jnp.where(mask > 0.5, rank, -1)
    order = jnp.zeros((count, count), jnp.int32)
    for place in range(SLOTS):
        tile = jnp.sum(jnp.where(slot == place, second, 0), axis=1, keepdims=True)
        order = jnp.where(second == place, tile, order)
    ones = jnp.sum((slot >= 0).astype(jnp.int32), axis=1, keepdims=True)
    order = jnp.where(second == SLOTS, ones, order)
    table_ref[:, :count] = slot
    table_ref[:, count:] = order


def tables(pattern, tile_perm):
    count = pattern.shape[0]
    shape = jax.ShapeDtypeStruct((count, 2 * count), jnp.int32)
    return call(table_kernel, shape, (pattern, tile_perm[:, None]), tables=0)


def place_of(row):
    return row // 4, (row // 2) % 2, row % 2


def pack_kernel(table_ref, strips_ref, packed_ref):
    count = table_ref.shape[0]
    row = lax.axis_index("row")
    per_col = strips_ref.shape[2] // TILE
    ones = table_ref[row, count + SLOTS]
    for place in range(SLOTS):
        tile = table_ref[row, count + place]
        start = pl.multiple_of((tile % per_col) * TILE, TILE)
        block = strips_ref[tile // per_col, :, pl.ds(start, TILE)]
        packed_ref[:, place * TILE : (place + 1) * TILE] = jnp.where(
            place < ones, block, jnp.zeros_like(block)
        )


def pack(table, strips):
    shape = jax.ShapeDtypeStruct((strips.shape[1], SLOTS * TILE), strips.dtype)
    return call(pack_kernel, shape, (table, strips), limit=8)


def fill(table_ref, factor_ref, blocks, places):
    count = table_ref.shape[0]
    depth = factor_ref.shape[0] // SLOTS
    row = lax.axis_index("row")
    z, y_hi, core = place_of(row)
    ones = table_ref[row, count + SLOTS]
    for block, (step, y_flip, core_flip) in zip(blocks, places):
        passed_by = core ^ core_flip
        z_of = (z + Z + step * (2 * passed_by - 1)) % Z
        for half in range(block.shape[0] // depth):
            other = (z_of * Y_HI + (y_hi ^ y_flip)) * CORE + (passed_by ^ half)
            place = table_ref[row, other]

            @pl.when(place >= 0)
            def _(block=block, half=half, other=other, place=place):
                start = pl.multiple_of(place * depth, depth)

                def copy(inner, _):
                    slot = table_ref[other, table_ref[row, count + inner]]

                    @pl.when(slot >= 0)
                    def _():
                        factor_ref[
                            pl.ds(start, depth), pl.ds(pl.multiple_of(inner * TILE, TILE), TILE)
                        ] = block[
                            half * depth : (half + 1) * depth,
                            pl.ds(pl.multiple_of(slot * TILE, TILE), TILE),
                        ]

                    return 0

                lax.fori_loop(0, ones, copy, 0)


def first_kernel(table_ref, *refs, places):
    refs[-1][...] = jnp.zeros_like(refs[-1])
    fill(table_ref, refs[-1], refs[:-1], places)


def next_kernel(table_ref, _, *refs, places):
    fill(table_ref, refs[-1], refs[:-1], places)


def grow(table, factor, arrived, depth):
    blocks, places = zip(*arrived)
    width = blocks[0].shape[1]
    shape = jax.ShapeDtypeStruct((SLOTS * depth, width), blocks[0].dtype)
    if factor is None:
        kernel = functools.partial(first_kernel, places=places)
        return call(kernel, shape, (table, *blocks), limit=8)
    kernel = functools.partial(next_kernel, places=places)
    return call(kernel, shape, (table, factor, *blocks), limit=8, input_output_aliases={1: 0})


def join_kernel(own_ref, other_ref, band_ref):
    depth = own_ref.shape[0] // X
    col = lax.axis_index("col")
    y_lo, x = col // X, col % X
    step = 1 - 2 * place_of(lax.axis_index("row"))[2]
    for ref, y_of in ((own_ref, y_lo), (other_ref, 1 - y_lo)):
        for index, x_step in enumerate((0, -step, step, 2)):
            strip = y_of * X + (x + X + x_step) % X
            band_ref[pl.ds(pl.multiple_of(strip * depth, depth), depth), :] = ref[
                index * depth : (index + 1) * depth, :
            ]


def join(own, other):
    rows, width = own.shape
    shape = jax.ShapeDtypeStruct((2 * rows, width), own.dtype)
    return call(join_kernel, shape, (own, other), tables=0, limit=8)


def square_kernel(table_ref, _, band_ref, *refs, places):
    blocks, (spread_ref, square_ref, factor_ref) = refs[:-3], refs[-3:]
    fill(table_ref, factor_ref, blocks, places)
    square = lax.dot_general(
        factor_ref[...],
        band_ref[...],
        (((1,), (1,)), ((), ())),
        preferred_element_type=jnp.float32,
    )
    square_ref[...] = square
    half = square.astype(jnp.bfloat16)
    for col in range(COL):
        spread_ref[col] = half


def square_strips(table, factor, band, arrived):
    blocks, places = zip(*arrived)
    rows = factor.shape[0]
    shapes = (
        jax.ShapeDtypeStruct((COL, rows, TILE), jnp.bfloat16),
        jax.ShapeDtypeStruct((rows, TILE), jnp.float32),
        jax.ShapeDtypeStruct(factor.shape, factor.dtype),
    )
    return call(
        functools.partial(square_kernel, places=places),
        shapes,
        (table, factor, band, *blocks),
        input_output_aliases={1: 2},
    )


def code(values, coded_ref, to, first):
    rows = values.shape[0]
    largest = jnp.max(jnp.abs(values), axis=0, keepdims=True)
    exponent = jnp.floor(jnp.log2(jnp.maximum(largest, 2.0**-100)))
    steps = jnp.round(values * jnp.exp2(14.0 - exponent))
    steps = jnp.clip(steps, -32767.0, 32767.0)
    coded_ref[to, first : first + rows, :] = steps.astype(jnp.int32).astype(jnp.int16)
    return jnp.broadcast_to(exponent, (8, values.shape[1]))


def cube_kernel(table_ref, factor_ref, square_ref, got_ref, coded_ref, whole, total, *, scale):
    count = table_ref.shape[0]
    row = lax.axis_index("row")
    cols, rows, _ = got_ref.shape
    depth = rows // SLOTS
    for strip in range(cols):
        for place in range(SLOTS):
            start = place * TILE + strip * depth
            whole[start : start + depth, :] = got_ref[
                strip, place * depth : (place + 1) * depth, :
            ]
    total[...] = scale * jnp.dot(
        factor_ref[...], whole[...], preferred_element_type=jnp.float32
    )
    per_col = count // cols
    for to in range(cols):
        marks = []
        for index, source in enumerate((total, square_ref)):
            values = []
            for spot in range(per_col):
                place = table_ref[row, to * per_col + spot]
                start = pl.multiple_of(jnp.maximum(place, 0) * depth, depth)
                values.append(jnp.where(place >= 0, source[pl.ds(start, depth), :], 0.0))
            values = jnp.concatenate(values, axis=0)
            marks.append(code(values, coded_ref, to, index * per_col * depth))
        marks = jnp.concatenate(marks, axis=0)
        coded_ref[to, 2 * per_col * depth :, :] = marks.astype(jnp.int32).astype(jnp.int16)


def cube_strips(table, factor, square, got, scale):
    cols, rows, _ = got.shape
    depth = rows // SLOTS
    per_col = table.shape[0] // cols
    shape = jax.ShapeDtypeStruct((cols, 2 * per_col * depth + 16, TILE), jnp.int16)
    return call(
        functools.partial(cube_kernel, scale=scale),
        shape,
        (table, factor, square, got),
        scratch_shapes=[
            pltpu.VMEM((SLOTS * TILE, TILE), jnp.bfloat16),
            pltpu.VMEM((rows, TILE), jnp.float32),
        ],
    )


def home_kernel(got_ref, square_ref, cubed_ref, held):
    cols, rows, _ = got_ref.shape
    per_col = square_ref.shape[1] // TILE
    depth = TILE // cols
    sizes = []
    for strip in range(cols):
        marks = got_ref[strip, rows - 16 :, :].astype(jnp.int32).astype(jnp.float32)
        sizes.append(jnp.exp2(marks - 14.0))
    for index, out_ref in enumerate((cubed_ref, square_ref)):
        for spot in range(per_col):
            for strip in range(cols):
                start = (index * per_col + spot) * depth
                steps = got_ref[strip, start : start + depth, :].astype(jnp.int32)
                size = sizes[strip][index * 8 : index * 8 + 1, :]
                held[strip * depth : (strip + 1) * depth, :] = steps.astype(jnp.float32) * size
            out_ref[:, spot * TILE : (spot + 1) * TILE] = held[...].T


def home(got, shape):
    out = jax.ShapeDtypeStruct(shape, jnp.float32)
    return call(
        home_kernel,
        (out, out),
        (got,),
        tables=0,
        scratch_shapes=[pltpu.VMEM((TILE, TILE), jnp.float32)],
    )


def local(density, pattern, tile_perm):
    rows, columns = density.shape
    depth = rows // COL
    table = tables(pattern, tile_perm)
    strips = lax.all_to_all(density.reshape(COL, depth, columns), "col", 0, 0)
    packed = pack(table, strips)
    across = to_other_y(packed)
    near = [jnp.concatenate([packed, to_other_core(packed)], 0)]
    far = [jnp.concatenate([across, to_other_core(across)], 0)]

    near.append(along_z(near[0]))
    far.append(along_z(far[0]))
    next_x = along_x(near[0])
    own = jnp.concatenate(
        [packed, next_x[:depth], to_other_core(next_x[depth:]), along_x(next_x[:depth])], 0
    )
    other = to_other_y_lo(own)
    near.append(along_z(near[1]))
    far.append(along_z(far[1]))
    near_swapped, far_swapped = [None], [None]

    def swap(block, swapped, hold):
        hold, arrived = lax.optimization_barrier((hold, to_other_core(block)))
        swapped.append(arrived)
        return hold

    near[2] = swap(near[1], near_swapped, near[2])
    near.append(along_z(near[2]))
    far[2] = swap(far[1], far_swapped, far[2])
    far.append(along_z(far[2]))
    near[3] = swap(near[2], near_swapped, near[3])

    def both(step, y_flip):
        direct, swapped = (far, far_swapped) if y_flip else (near, near_swapped)
        return [(direct[step], (step, y_flip, 0)), (swapped[step], (step, y_flip, 1))]

    factor = grow(table, None, [(near[0], (0, 0, 0)), (far[0], (0, 1, 0))] + both(1, 0), depth)
    near[3], factor = lax.optimization_barrier((near[3], factor))
    near.append(along_z(near[3][:depth]))
    far[3] = swap(far[2], far_swapped, far[3])
    near[4], far[3] = lax.optimization_barrier((near[4], far[3]))
    far.append(along_z(far[3][:depth]))
    factor = grow(table, factor, both(1, 1) + both(2, 0), depth)
    for step in (3, 4):
        near_swapped.append(to_other_core(near[step]))
    far_swapped.append(to_other_core(far[3]))
    factor = grow(table, factor, both(2, 1) + both(3, 0), depth)
    band = join(own, other)
    far[4], factor, band = lax.optimization_barrier((far[4], factor, band))
    far_swapped.append(to_other_core(far[4]))
    spread, square, factor = square_strips(
        table, factor, band, both(3, 1) + both(4, 0) + both(4, 1)
    )
    got = lax.all_to_all(spread, "col", 0, 0)
    scale = (rows * lax.axis_size("row") / 2.0) ** (-0.25)
    coded = cube_strips(table, factor, square, got, scale)
    return home(lax.all_to_all(coded, "col", 0, 0), (rows, columns))


def solution(mesh):
    return jax.shard_map(
        local,
        mesh=mesh,
        in_specs=(P("row", "col"), P(), P()),
        out_specs=(P("row", "col"), P("row", "col")),
        check_vma=False,
    )
```

```python
import functools

import jax
import jax.numpy as jnp
from jax import lax
from jax.experimental import pallas as pl
from jax.experimental.pallas import tpu as pltpu
from jax.sharding import PartitionSpec as P

TILE = 256
SLOTS = 13
BOTH = ("row", "col")
MIB = 1024 * 1024
VMEM = pl.BlockSpec(memory_space=pltpu.VMEM)
SMEM = pl.BlockSpec(memory_space=pltpu.SMEM)

Z, Y_HI, CORE, COL, X = 8, 2, 2, 8, 4


def device(z, y_hi, core, col):
    return ((z % Z * Y_HI + y_hi % Y_HI) * CORE + core % CORE) * COL + col


def pairs(move):
    places = [
        (z, y_hi, core, col)
        for z in range(Z)
        for y_hi in range(Y_HI)
        for core in range(CORE)
        for col in range(COL)
    ]
    return [(device(*place), device(*move(*place))) for place in places]


def move(block, place):
    return lax.ppermute(block, BOTH, pairs(place))


def to_other_core(block):
    return move(block, lambda z, y, core, col: (z, y, core + 1, col))


def to_other_y(block):
    return move(block, lambda z, y, core, col: (z, y + 1, core, col))


def to_other_y_lo(block):
    return move(block, lambda z, y, core, col: (z, y, core, (col + X) % COL))


def along_x(block):
    return move(
        block,
        lambda z, y, core, col: (z, y, core, col // X * X + (col + 1 - 2 * core) % X),
    )


def along_z(block, steps=1):
    return move(block, lambda z, y, core, col: (z + steps * (1 - 2 * core), y, core, col))


def call(kernel, out_shape, operands, tables=1, limit=16, **options):
    return pl.pallas_call(
        kernel,
        out_shape=out_shape,
        in_specs=[SMEM] * tables + [VMEM] * (len(operands) - tables),
        out_specs=jax.tree.map(lambda _: VMEM, out_shape),
        compiler_params=pltpu.CompilerParams(vmem_limit_bytes=limit * MIB),
        **options,
    )(*operands)


def table_kernel(pattern_ref, perm_ref, table_ref):
    count = pattern_ref.shape[0]
    first = lax.broadcasted_iota(jnp.int32, (count, count), 0)
    second = lax.broadcasted_iota(jnp.int32, (count, count), 1)
    pattern = pattern_ref[...].astype(jnp.float32)
    one_hot = (perm_ref[...] == second).astype(jnp.float32)
    upper = jnp.where(first <= second, pattern, 0.0)
    strict = jnp.where(first < second, pattern, 0.0)

    def dot(a, b, b_dim):
        return lax.dot_general(
            a, b, (((1,), (b_dim,)), ((), ())), preferred_element_type=jnp.float32
        )

    mask = dot(dot(one_hot, upper, 0) + dot(one_hot, strict, 1), one_hot, 1)
    rank = dot(mask, (first < second).astype(jnp.float32), 0).astype(jnp.int32)
    slot = jnp.where(mask > 0.5, rank, -1)
    order = jnp.zeros((count, count), jnp.int32)
    for place in range(SLOTS):
        tile = jnp.sum(jnp.where(slot == place, second, 0), axis=1, keepdims=True)
        order = jnp.where(second == place, tile, order)
    ones = jnp.sum((slot >= 0).astype(jnp.int32), axis=1, keepdims=True)
    order = jnp.where(second == SLOTS, ones, order)
    table_ref[:, :count] = slot
    table_ref[:, count:] = order


def tables(pattern, tile_perm):
    count = pattern.shape[0]
    shape = jax.ShapeDtypeStruct((count, 2 * count), jnp.int32)
    return call(table_kernel, shape, (pattern, tile_perm[:, None]), tables=0)


def place_of(row):
    return row // 4, (row // 2) % 2, row % 2


def pack_kernel(table_ref, strips_ref, packed_ref):
    count = table_ref.shape[0]
    row = lax.axis_index("row")
    per_col = strips_ref.shape[2] // TILE
    ones = table_ref[row, count + SLOTS]
    for place in range(SLOTS):
        tile = table_ref[row, count + place]
        start = pl.multiple_of((tile % per_col) * TILE, TILE)
        block = strips_ref[tile // per_col, :, pl.ds(start, TILE)]
        packed_ref[:, place * TILE : (place + 1) * TILE] = jnp.where(
            place < ones, block, jnp.zeros_like(block)
        )


def pack(table, strips):
    shape = jax.ShapeDtypeStruct((strips.shape[1], SLOTS * TILE), strips.dtype)
    return call(pack_kernel, shape, (table, strips), limit=8)


def fill(table_ref, factor_ref, blocks, places):
    count = table_ref.shape[0]
    depth = factor_ref.shape[0] // SLOTS
    row = lax.axis_index("row")
    z, y_hi, core = place_of(row)
    ones = table_ref[row, count + SLOTS]
    for block, (step, y_flip, core_flip) in zip(blocks, places):
        passed_by = core ^ core_flip
        z_of = (z + Z + step * (2 * passed_by - 1)) % Z
        for half in range(block.shape[0] // depth):
            other = (z_of * Y_HI + (y_hi ^ y_flip)) * CORE + (passed_by ^ half)
            place = table_ref[row, other]

            @pl.when(place >= 0)
            def _(block=block, half=half, other=other, place=place):
                start = pl.multiple_of(place * depth, depth)

                def copy(inner, _):
                    slot = table_ref[other, table_ref[row, count + inner]]

                    @pl.when(slot >= 0)
                    def _():
                        factor_ref[
                            pl.ds(start, depth), pl.ds(pl.multiple_of(inner * TILE, TILE), TILE)
                        ] = block[
                            half * depth : (half + 1) * depth,
                            pl.ds(pl.multiple_of(slot * TILE, TILE), TILE),
                        ]

                    return 0

                lax.fori_loop(0, ones, copy, 0)


def first_kernel(table_ref, *refs, places):
    refs[-1][...] = jnp.zeros_like(refs[-1])
    fill(table_ref, refs[-1], refs[:-1], places)


def next_kernel(table_ref, _, *refs, places):
    fill(table_ref, refs[-1], refs[:-1], places)


def grow(table, factor, arrived, depth):
    blocks, places = zip(*arrived)
    width = blocks[0].shape[1]
    shape = jax.ShapeDtypeStruct((SLOTS * depth, width), blocks[0].dtype)
    if factor is None:
        kernel = functools.partial(first_kernel, places=places)
        return call(kernel, shape, (table, *blocks), limit=8)
    kernel = functools.partial(next_kernel, places=places)
    return call(kernel, shape, (table, factor, *blocks), limit=8, input_output_aliases={1: 0})


def join_kernel(own_ref, far_own_ref, other_ref, far_other_ref, band_ref):
    depth = own_ref.shape[0] // 2
    col = lax.axis_index("col")
    y_lo, x = col // X, col % X
    step = 1 - 2 * place_of(lax.axis_index("row"))[2]
    for ref, y_of, x_steps in (
        (own_ref, y_lo, (0, -step)),
        (far_own_ref, y_lo, (step, 2)),
        (other_ref, 1 - y_lo, (0, -step)),
        (far_other_ref, 1 - y_lo, (step, 2)),
    ):
        for index, x_step in enumerate(x_steps):
            strip = y_of * X + (x + X + x_step) % X
            band_ref[pl.ds(pl.multiple_of(strip * depth, depth), depth), :] = ref[
                index * depth : (index + 1) * depth, :
            ]


def join(*pieces):
    rows, width = pieces[0].shape
    shape = jax.ShapeDtypeStruct((4 * rows, width), pieces[0].dtype)
    return call(join_kernel, shape, pieces, tables=0, limit=8)


MARKS = 16


def code(strips):
    steps, marks = [], []
    for values in strips:
        largest = jnp.max(jnp.abs(values), axis=0, keepdims=True)
        exponent = jnp.floor(jnp.log2(jnp.maximum(largest, 2.0**-100)))
        scaled = jnp.round(values * jnp.exp2(14.0 - exponent))
        steps.append(jnp.clip(scaled, -32767.0, 32767.0))
        marks.append(exponent)
    marks += [jnp.zeros_like(marks[0])] * (MARKS - len(marks))
    coded = jnp.concatenate(steps + marks, axis=0)
    return coded.astype(jnp.int32).astype(jnp.int16)


def steps_of(coded_ref, strip):
    first = coded_ref.shape[1] - MARKS
    marks = coded_ref[strip, first:, :].astype(jnp.int32).astype(jnp.float32)
    return jnp.exp2(marks - 14.0)


def decode(steps, step):
    return steps.astype(jnp.int32).astype(jnp.float32) * step


def square_kernel(table_ref, _, band_ref, *refs, places):
    blocks, (spread_ref, factor_ref) = refs[:-2], refs[-2:]
    fill(table_ref, factor_ref, blocks, places)
    square = lax.dot_general(
        factor_ref[...],
        band_ref[...],
        (((1,), (1,)), ((), ())),
        preferred_element_type=jnp.float32,
    )
    depth = square.shape[0] // SLOTS
    coded = code([square[place * depth : (place + 1) * depth] for place in range(SLOTS)])
    for col in range(COL):
        spread_ref[col] = coded


def square_strips(table, factor, band, arrived):
    blocks, places = zip(*arrived)
    shapes = (
        jax.ShapeDtypeStruct((COL, factor.shape[0] + MARKS, TILE), jnp.int16),
        jax.ShapeDtypeStruct(factor.shape, factor.dtype),
    )
    return call(
        functools.partial(square_kernel, places=places),
        shapes,
        (table, factor, band, *blocks),
        input_output_aliases={1: 1},
    )


def cube_kernel(table_ref, factor_ref, got_ref, coded_ref, whole, total, *, scale):
    count = table_ref.shape[0]
    row = lax.axis_index("row")
    cols, rows, _ = got_ref.shape
    depth = (rows - MARKS) // SLOTS
    for strip in range(cols):
        sizes = steps_of(got_ref, strip)
        for place in range(SLOTS):
            start = place * TILE + strip * depth
            steps = got_ref[strip, place * depth : (place + 1) * depth, :]
            square = decode(steps, sizes[place : place + 1])
            whole[start : start + depth, :] = square.astype(jnp.bfloat16)
    total[...] = scale * jnp.dot(
        factor_ref[...], whole[...], preferred_element_type=jnp.float32
    )
    per_col = count // cols
    for to in range(cols):
        values = []
        for spot in range(per_col):
            place = table_ref[row, to * per_col + spot]
            start = pl.multiple_of(jnp.maximum(place, 0) * depth, depth)
            values.append(jnp.where(place >= 0, total[pl.ds(start, depth), :], 0.0))
        coded_ref[to] = code(values)


def cube_strips(table, factor, got, scale):
    cols, rows, _ = got.shape
    depth = (rows - MARKS) // SLOTS
    per_col = table.shape[0] // cols
    shape = jax.ShapeDtypeStruct((cols, per_col * depth + MARKS, TILE), jnp.int16)
    return call(
        functools.partial(cube_kernel, scale=scale),
        shape,
        (table, factor, got),
        scratch_shapes=[
            pltpu.VMEM((SLOTS * TILE, TILE), jnp.bfloat16),
            pltpu.VMEM((SLOTS * depth, TILE), jnp.float32),
        ],
    )


def square_home_kernel(table_ref, got_ref, square_ref, held):
    row, col = lax.axis_index("row"), lax.axis_index("col")
    cols, rows, _ = got_ref.shape
    depth = (rows - MARKS) // SLOTS
    per_col = square_ref.shape[1] // TILE
    sizes = [steps_of(got_ref, strip) for strip in range(cols)]
    index = lax.broadcasted_iota(jnp.int32, sizes[0].shape, 0)
    for spot in range(per_col):
        place = table_ref[row, col * per_col + spot]
        start = pl.multiple_of(jnp.maximum(place, 0) * depth, depth)
        for strip in range(cols):
            size = jnp.sum(jnp.where(index == place, sizes[strip], 0.0), axis=0, keepdims=True)
            held[strip * depth : (strip + 1) * depth, :] = decode(
                got_ref[strip, pl.ds(start, depth), :], size
            )
        square_ref[:, spot * TILE : (spot + 1) * TILE] = held[...].T


def cube_home_kernel(got_ref, cubed_ref, held):
    cols = got_ref.shape[0]
    depth = TILE // cols
    sizes = [steps_of(got_ref, strip) for strip in range(cols)]
    for spot in range(cubed_ref.shape[1] // TILE):
        for strip in range(cols):
            steps = got_ref[strip, spot * depth : (spot + 1) * depth, :]
            held[strip * depth : (strip + 1) * depth, :] = decode(
                steps, sizes[strip][spot : spot + 1]
            )
        cubed_ref[:, spot * TILE : (spot + 1) * TILE] = held[...].T


def home(kernel, operands, tables, shape):
    out = jax.ShapeDtypeStruct(shape, jnp.float32)
    scratch = [pltpu.VMEM((TILE, TILE), jnp.float32)]
    return call(kernel, out, operands, tables=tables, scratch_shapes=scratch)


def local(density, pattern, tile_perm):
    rows, columns = density.shape
    depth = rows // COL
    table = tables(pattern, tile_perm)
    strips = lax.all_to_all(density.reshape(COL, depth, columns), "col", 0, 0)
    packed = pack(table, strips)
    across = to_other_y(packed)
    near = [jnp.concatenate([packed, to_other_core(packed)], 0)]
    far = [jnp.concatenate([across, to_other_core(across)], 0)]

    near.append(along_z(near[0]))
    far.append(along_z(far[0]))
    next_x = along_x(near[0])
    own = jnp.concatenate([packed, next_x[:depth]], 0)
    other = to_other_y_lo(own)
    far_own = jnp.concatenate([to_other_core(next_x[depth:]), along_x(next_x[:depth])], 0)
    far_other = to_other_y_lo(far_own)
    near.append(along_z(near[1]))
    far.append(along_z(far[1]))
    near_swapped, far_swapped = [None], [None]

    def swap(block, swapped, hold):
        hold, arrived = lax.optimization_barrier((hold, to_other_core(block)))
        swapped.append(arrived)
        return hold

    near[2] = swap(near[1], near_swapped, near[2])
    near.append(along_z(near[2]))
    far[2] = swap(far[1], far_swapped, far[2])
    far[2], other = lax.optimization_barrier((far[2], other))
    far.append(along_z(far[2]))
    near[3] = swap(near[2], near_swapped, near[3])

    def both(step, y_flip):
        direct, swapped = (far, far_swapped) if y_flip else (near, near_swapped)
        return [(direct[step], (step, y_flip, 0)), (swapped[step], (step, y_flip, 1))]

    factor = grow(table, None, [(near[0], (0, 0, 0)), (far[0], (0, 1, 0))] + both(1, 0), depth)
    near[3], factor = lax.optimization_barrier((near[3], factor))
    near.append(along_z(near[3][:depth]))
    far[3] = swap(far[2], far_swapped, far[3])
    far.append(along_z(far[3][:depth]))
    factor = grow(table, factor, both(1, 1) + both(2, 0), depth)
    for step in (3, 4):
        near_swapped.append(to_other_core(near[step]))
    far_swapped.append(to_other_core(far[3]))
    factor = grow(table, factor, both(2, 1) + both(3, 0), depth)
    band = join(own, far_own, other, far_other)
    far[4], factor, band = lax.optimization_barrier((far[4], factor, band))
    far_swapped.append(to_other_core(far[4]))
    spread, factor = square_strips(
        table, factor, band, both(3, 1) + both(4, 0) + both(4, 1)
    )
    got = lax.all_to_all(spread, "col", 0, 0)
    scale = (rows * lax.axis_size("row") / 2.0) ** (-0.25)
    coded = cube_strips(table, factor, got, scale)
    square = home(square_home_kernel, (table, got), 1, (rows, columns))
    cubed = home(cube_home_kernel, (lax.all_to_all(coded, "col", 0, 0),), 0, (rows, columns))
    return square, cubed


def solution(mesh):
    return jax.shard_map(
        local,
        mesh=mesh,
        in_specs=(P("row", "col"), P(), P()),
        out_specs=(P("row", "col"), P("row", "col")),
        check_vma=False,
    )
```

```python
import functools

import jax
import jax.numpy as jnp
from jax import lax
from jax.experimental import pallas as pl
from jax.experimental.pallas import tpu as pltpu
from jax.sharding import PartitionSpec as P

TILE = 256
SLOTS = 13
BOTH = ("row", "col")
MIB = 1024 * 1024
VMEM = pl.BlockSpec(memory_space=pltpu.VMEM)
SMEM = pl.BlockSpec(memory_space=pltpu.SMEM)

Z, Y_HI, CORE, COL, X = 8, 2, 2, 8, 4


def device(z, y_hi, core, col):
    return ((z % Z * Y_HI + y_hi % Y_HI) * CORE + core % CORE) * COL + col


def pairs(move):
    places = [
        (z, y_hi, core, col)
        for z in range(Z)
        for y_hi in range(Y_HI)
        for core in range(CORE)
        for col in range(COL)
    ]
    return [(device(*place), device(*move(*place))) for place in places]


def move(block, place):
    return lax.ppermute(block, BOTH, pairs(place))


def to_other_core(block):
    return move(block, lambda z, y, core, col: (z, y, core + 1, col))


def to_other_y(block):
    return move(block, lambda z, y, core, col: (z, y + 1, core, col))


def to_other_y_lo(block):
    return move(block, lambda z, y, core, col: (z, y, core, (col + X) % COL))


def along_x(block):
    return move(
        block,
        lambda z, y, core, col: (z, y, core, col // X * X + (col + 1 - 2 * core) % X),
    )


def along_z(block, steps=1):
    return move(block, lambda z, y, core, col: (z + steps * (1 - 2 * core), y, core, col))


def call(kernel, out_shape, operands, tables=1, limit=16, **options):
    return pl.pallas_call(
        kernel,
        out_shape=out_shape,
        in_specs=[SMEM] * tables + [VMEM] * (len(operands) - tables),
        out_specs=jax.tree.map(lambda _: VMEM, out_shape),
        compiler_params=pltpu.CompilerParams(vmem_limit_bytes=limit * MIB),
        **options,
    )(*operands)


def table_kernel(pattern_ref, perm_ref, table_ref):
    count = pattern_ref.shape[0]
    first = lax.broadcasted_iota(jnp.int32, (count, count), 0)
    second = lax.broadcasted_iota(jnp.int32, (count, count), 1)
    pattern = pattern_ref[...].astype(jnp.float32)
    one_hot = (perm_ref[...] == second).astype(jnp.float32)
    upper = jnp.where(first <= second, pattern, 0.0)
    strict = jnp.where(first < second, pattern, 0.0)

    def dot(a, b, b_dim):
        return lax.dot_general(
            a, b, (((1,), (b_dim,)), ((), ())), preferred_element_type=jnp.float32
        )

    mask = dot(dot(one_hot, upper, 0) + dot(one_hot, strict, 1), one_hot, 1)
    rank = dot(mask, (first < second).astype(jnp.float32), 0).astype(jnp.int32)
    slot = jnp.where(mask > 0.5, rank, -1)
    order = jnp.zeros((count, count), jnp.int32)
    for place in range(SLOTS):
        tile = jnp.sum(jnp.where(slot == place, second, 0), axis=1, keepdims=True)
        order = jnp.where(second == place, tile, order)
    ones = jnp.sum((slot >= 0).astype(jnp.int32), axis=1, keepdims=True)
    order = jnp.where(second == SLOTS, ones, order)
    table_ref[:, :count] = slot
    table_ref[:, count:] = order


def tables(pattern, tile_perm):
    count = pattern.shape[0]
    shape = jax.ShapeDtypeStruct((count, 2 * count), jnp.int32)
    return call(table_kernel, shape, (pattern, tile_perm[:, None]), tables=0)


def place_of(row):
    return row // 4, (row // 2) % 2, row % 2


def pack_kernel(table_ref, strips_ref, packed_ref):
    count = table_ref.shape[0]
    row = lax.axis_index("row")
    per_col = strips_ref.shape[2] // TILE
    ones = table_ref[row, count + SLOTS]
    for place in range(SLOTS):
        tile = table_ref[row, count + place]
        start = pl.multiple_of((tile % per_col) * TILE, TILE)
        block = strips_ref[tile // per_col, :, pl.ds(start, TILE)]
        packed_ref[:, place * TILE : (place + 1) * TILE] = jnp.where(
            place < ones, block, jnp.zeros_like(block)
        )


def pack(table, strips):
    shape = jax.ShapeDtypeStruct((strips.shape[1], SLOTS * TILE), strips.dtype)
    return call(pack_kernel, shape, (table, strips), limit=8)


def fill(table_ref, factor_ref, blocks, places):
    count = table_ref.shape[0]
    depth = factor_ref.shape[0] // SLOTS
    row = lax.axis_index("row")
    z, y_hi, core = place_of(row)
    ones = table_ref[row, count + SLOTS]
    for block, (step, y_flip, core_flip) in zip(blocks, places):
        passed_by = core ^ core_flip
        z_of = (z + Z + step * (2 * passed_by - 1)) % Z
        for half in range(block.shape[0] // depth):
            other = (z_of * Y_HI + (y_hi ^ y_flip)) * CORE + (passed_by ^ half)
            place = table_ref[row, other]

            @pl.when(place >= 0)
            def _(block=block, half=half, other=other, place=place):
                start = pl.multiple_of(place * depth, depth)

                def copy(inner, _):
                    slot = table_ref[other, table_ref[row, count + inner]]

                    @pl.when(slot >= 0)
                    def _():
                        factor_ref[
                            pl.ds(start, depth), pl.ds(pl.multiple_of(inner * TILE, TILE), TILE)
                        ] = block[
                            half * depth : (half + 1) * depth,
                            pl.ds(pl.multiple_of(slot * TILE, TILE), TILE),
                        ]

                    return 0

                lax.fori_loop(0, ones, copy, 0)


def first_kernel(table_ref, *refs, places):
    refs[-1][...] = jnp.zeros_like(refs[-1])
    fill(table_ref, refs[-1], refs[:-1], places)


def next_kernel(table_ref, _, *refs, places):
    fill(table_ref, refs[-1], refs[:-1], places)


def grow(table, factor, arrived, depth):
    blocks, places = zip(*arrived)
    width = blocks[0].shape[1]
    shape = jax.ShapeDtypeStruct((SLOTS * depth, width), blocks[0].dtype)
    if factor is None:
        kernel = functools.partial(first_kernel, places=places)
        return call(kernel, shape, (table, *blocks), limit=8)
    kernel = functools.partial(next_kernel, places=places)
    return call(kernel, shape, (table, factor, *blocks), limit=8, input_output_aliases={1: 0})


def join_kernel(own_ref, far_own_ref, other_ref, far_other_ref, band_ref):
    depth = own_ref.shape[0] // 2
    col = lax.axis_index("col")
    y_lo, x = col // X, col % X
    step = 1 - 2 * place_of(lax.axis_index("row"))[2]
    for ref, y_of, x_steps in (
        (own_ref, y_lo, (0, -step)),
        (far_own_ref, y_lo, (step, 2)),
        (other_ref, 1 - y_lo, (0, -step)),
        (far_other_ref, 1 - y_lo, (step, 2)),
    ):
        for index, x_step in enumerate(x_steps):
            strip = y_of * X + (x + X + x_step) % X
            band_ref[pl.ds(pl.multiple_of(strip * depth, depth), depth), :] = ref[
                index * depth : (index + 1) * depth, :
            ]


def join(*pieces):
    rows, width = pieces[0].shape
    shape = jax.ShapeDtypeStruct((4 * rows, width), pieces[0].dtype)
    return call(join_kernel, shape, pieces, tables=0, limit=8)


MARKS = 16


def code(strips):
    steps, marks = [], []
    for values in strips:
        largest = jnp.max(jnp.abs(values), axis=0, keepdims=True)
        exponent = jnp.floor(jnp.log2(jnp.maximum(largest, 2.0**-100)))
        scaled = jnp.round(values * jnp.exp2(14.0 - exponent))
        steps.append(jnp.clip(scaled, -32767.0, 32767.0))
        marks.append(exponent)
    marks += [jnp.zeros_like(marks[0])] * (MARKS - len(marks))
    return jnp.concatenate(steps, axis=0), jnp.concatenate(marks, axis=0)


def to_16_bits(values):
    return values.astype(jnp.int32).astype(jnp.int16)


def steps_of(coded_ref, strip):
    first = coded_ref.shape[1] - MARKS
    marks = coded_ref[strip, first:, :].astype(jnp.int32).astype(jnp.float32)
    return jnp.exp2(marks - 14.0)


def decode(steps, step):
    return steps.astype(jnp.int32).astype(jnp.float32) * step


def square_kernel(table_ref, _, band_ref, *refs, places):
    blocks, (spread_ref, factor_ref) = refs[:-2], refs[-2:]
    fill(table_ref, factor_ref, blocks, places)
    square = lax.dot_general(
        factor_ref[...],
        band_ref[...],
        (((1,), (1,)), ((), ())),
        preferred_element_type=jnp.float32,
    )
    depth = square.shape[0] // SLOTS
    coded = code([square[place * depth : (place + 1) * depth] for place in range(SLOTS)])
    coded = to_16_bits(jnp.concatenate(coded, axis=0))
    for col in range(COL):
        spread_ref[col] = coded


def square_strips(table, factor, band, arrived):
    blocks, places = zip(*arrived)
    shapes = (
        jax.ShapeDtypeStruct((COL, factor.shape[0] + MARKS, TILE), jnp.int16),
        jax.ShapeDtypeStruct(factor.shape, factor.dtype),
    )
    return call(
        functools.partial(square_kernel, places=places),
        shapes,
        (table, factor, band, *blocks),
        input_output_aliases={1: 1},
    )


def cube_kernel(table_ref, factor_ref, got_ref, coded_ref, whole, held, held_marks, *, scale):
    count = table_ref.shape[0]
    row = lax.axis_index("row")
    cols, rows, _ = got_ref.shape
    depth = (rows - MARKS) // SLOTS
    for strip in range(cols):
        sizes = steps_of(got_ref, strip)
        for place in range(SLOTS):
            start = place * TILE + strip * depth
            steps = got_ref[strip, place * depth : (place + 1) * depth, :]
            square = decode(steps, sizes[place : place + 1])
            whole[start : start + depth, :] = square.astype(jnp.bfloat16)
    total = scale * jnp.dot(factor_ref[...], whole[...], preferred_element_type=jnp.float32)
    steps, marks = code([total[place * depth : (place + 1) * depth] for place in range(SLOTS)])
    held[...] = to_16_bits(steps)
    held_marks[...] = marks
    per_col = count // cols
    for to in range(cols):
        marks = []
        for spot in range(per_col):
            place = table_ref[row, to * per_col + spot]
            first = jnp.maximum(place, 0)
            block = held[pl.ds(pl.multiple_of(first * depth, depth), depth), :]
            coded_ref[to, spot * depth : (spot + 1) * depth, :] = jnp.where(
                place >= 0, block, jnp.zeros_like(block)
            )
            marks.append(held_marks[pl.ds(first, 1), :])
        marks += [jnp.zeros_like(marks[0])] * (MARKS - per_col)
        coded_ref[to, per_col * depth :, :] = to_16_bits(jnp.concatenate(marks, axis=0))


def cube_strips(table, factor, got, scale):
    cols, rows, _ = got.shape
    depth = (rows - MARKS) // SLOTS
    per_col = table.shape[0] // cols
    shape = jax.ShapeDtypeStruct((cols, per_col * depth + MARKS, TILE), jnp.int16)
    return call(
        functools.partial(cube_kernel, scale=scale),
        shape,
        (table, factor, got),
        scratch_shapes=[
            pltpu.VMEM((SLOTS * TILE, TILE), jnp.bfloat16),
            pltpu.VMEM((SLOTS * depth, TILE), jnp.int16),
            pltpu.VMEM((MARKS, TILE), jnp.float32),
        ],
    )


def square_home_kernel(table_ref, got_ref, square_ref, held):
    row, col = lax.axis_index("row"), lax.axis_index("col")
    cols, rows, _ = got_ref.shape
    depth = (rows - MARKS) // SLOTS
    per_col = square_ref.shape[1] // TILE
    sizes = [steps_of(got_ref, strip) for strip in range(cols)]
    index = lax.broadcasted_iota(jnp.int32, sizes[0].shape, 0)
    for spot in range(per_col):
        place = table_ref[row, col * per_col + spot]
        start = pl.multiple_of(jnp.maximum(place, 0) * depth, depth)
        for strip in range(cols):
            size = jnp.sum(jnp.where(index == place, sizes[strip], 0.0), axis=0, keepdims=True)
            held[strip * depth : (strip + 1) * depth, :] = decode(
                got_ref[strip, pl.ds(start, depth), :], size
            )
        square_ref[:, spot * TILE : (spot + 1) * TILE] = held[...].T


def cube_home_kernel(got_ref, cubed_ref, held):
    cols = got_ref.shape[0]
    depth = TILE // cols
    sizes = [steps_of(got_ref, strip) for strip in range(cols)]
    for spot in range(cubed_ref.shape[1] // TILE):
        for strip in range(cols):
            steps = got_ref[strip, spot * depth : (spot + 1) * depth, :]
            held[strip * depth : (strip + 1) * depth, :] = decode(
                steps, sizes[strip][spot : spot + 1]
            )
        cubed_ref[:, spot * TILE : (spot + 1) * TILE] = held[...].T


def home(kernel, operands, tables, shape):
    out = jax.ShapeDtypeStruct(shape, jnp.float32)
    scratch = [pltpu.VMEM((TILE, TILE), jnp.float32)]
    return call(kernel, out, operands, tables=tables, scratch_shapes=scratch)


def local(density, pattern, tile_perm):
    rows, columns = density.shape
    depth = rows // COL
    table = tables(pattern, tile_perm)
    strips = lax.all_to_all(density.reshape(COL, depth, columns), "col", 0, 0)
    packed = pack(table, strips)
    across = to_other_y(packed)
    near = [jnp.concatenate([packed, to_other_core(packed)], 0)]
    far = [jnp.concatenate([across, to_other_core(across)], 0)]

    far.append(along_z(far[0]))
    near.append(along_z(near[0]))
    next_x = along_x(near[0])
    own = jnp.concatenate([packed, next_x[:depth]], 0)
    other = to_other_y_lo(own)
    far_own = jnp.concatenate([to_other_core(next_x[depth:]), along_x(next_x[:depth])], 0)
    far_other = to_other_y_lo(far_own)
    far.append(along_z(far[1]))
    near.append(along_z(near[1]))
    near_swapped, far_swapped = [None], [None]

    def swap(block, swapped, hold):
        hold, arrived = lax.optimization_barrier((hold, to_other_core(block)))
        swapped.append(arrived)
        return hold

    near[2] = swap(near[1], near_swapped, near[2])
    near.append(along_z(near[2]))
    far[2] = swap(far[1], far_swapped, far[2])
    far[2], other = lax.optimization_barrier((far[2], other))
    far.append(along_z(far[2]))
    near[3] = swap(near[2], near_swapped, near[3])

    def both(step, y_flip):
        direct, swapped = (far, far_swapped) if y_flip else (near, near_swapped)
        return [(direct[step], (step, y_flip, 0)), (swapped[step], (step, y_flip, 1))]

    factor = grow(table, None, [(near[0], (0, 0, 0)), (far[0], (0, 1, 0))] + both(1, 0), depth)
    near[3], factor = lax.optimization_barrier((near[3], factor))
    near.append(along_z(near[3][:depth]))
    far_swapped.append(to_other_core(far[2]))
    far.append(along_z(far[3][:depth]))
    for step in (3, 4):
        near_swapped.append(to_other_core(near[step]))
    far_swapped.append(to_other_core(far[3]))
    factor = grow(table, factor, both(1, 1) + both(2, 0) + both(2, 1) + both(3, 0), depth)
    band = join(own, far_own, other, far_other)
    far[4], factor, band = lax.optimization_barrier((far[4], factor, band))
    far_swapped.append(to_other_core(far[4]))
    spread, factor = square_strips(
        table, factor, band, both(3, 1) + both(4, 0) + both(4, 1)
    )
    got = lax.all_to_all(spread, "col", 0, 0)
    scale = (rows * lax.axis_size("row") / 2.0) ** (-0.25)
    coded = cube_strips(table, factor, got, scale)
    square = home(square_home_kernel, (table, got), 1, (rows, columns))
    cubed = home(cube_home_kernel, (lax.all_to_all(coded, "col", 0, 0),), 0, (rows, columns))
    return square, cubed


def solution(mesh):
    return jax.shard_map(
        local,
        mesh=mesh,
        in_specs=(P("row", "col"), P(), P()),
        out_specs=(P("row", "col"), P("row", "col")),
        check_vma=False,
    )
```

```python
import functools

import jax
import jax.numpy as jnp
from jax import lax
from jax.experimental import pallas as pl
from jax.experimental.pallas import tpu as pltpu
from jax.sharding import PartitionSpec as P

TILE = 256
SLOTS = 13
BOTH = ("row", "col")
MIB = 1024 * 1024
VMEM = pl.BlockSpec(memory_space=pltpu.VMEM)
SMEM = pl.BlockSpec(memory_space=pltpu.SMEM)

Z, Y_HI, CORE, COL, X = 8, 2, 2, 8, 4


def device(z, y_hi, core, col):
    return ((z % Z * Y_HI + y_hi % Y_HI) * CORE + core % CORE) * COL + col


def pairs(move):
    places = [
        (z, y_hi, core, col)
        for z in range(Z)
        for y_hi in range(Y_HI)
        for core in range(CORE)
        for col in range(COL)
    ]
    return [(device(*place), device(*move(*place))) for place in places]


def move(block, place):
    return lax.ppermute(block, BOTH, pairs(place))


def to_other_core(block):
    return move(block, lambda z, y, core, col: (z, y, core + 1, col))


def to_other_y(block):
    return move(block, lambda z, y, core, col: (z, y + 1, core, col))


def to_other_y_lo(block):
    return move(block, lambda z, y, core, col: (z, y, core, (col + X) % COL))


def along_x(block):
    return move(
        block,
        lambda z, y, core, col: (z, y, core, col // X * X + (col + 1 - 2 * core) % X),
    )


def along_z(block, steps=1):
    return move(block, lambda z, y, core, col: (z + steps * (1 - 2 * core), y, core, col))


def call(kernel, out_shape, operands, tables=1, limit=16, **options):
    return pl.pallas_call(
        kernel,
        out_shape=out_shape,
        in_specs=[SMEM] * tables + [VMEM] * (len(operands) - tables),
        out_specs=jax.tree.map(lambda _: VMEM, out_shape),
        compiler_params=pltpu.CompilerParams(vmem_limit_bytes=limit * MIB),
        **options,
    )(*operands)


def table_kernel(pattern_ref, perm_ref, table_ref):
    count = pattern_ref.shape[0]
    first = lax.broadcasted_iota(jnp.int32, (count, count), 0)
    second = lax.broadcasted_iota(jnp.int32, (count, count), 1)
    pattern = pattern_ref[...].astype(jnp.float32)
    one_hot = (perm_ref[...] == second).astype(jnp.float32)
    upper = jnp.where(first <= second, pattern, 0.0)
    strict = jnp.where(first < second, pattern, 0.0)

    def dot(a, b, b_dim):
        return lax.dot_general(
            a, b, (((1,), (b_dim,)), ((), ())), preferred_element_type=jnp.float32
        )

    mask = dot(dot(one_hot, upper, 0) + dot(one_hot, strict, 1), one_hot, 1)
    rank = dot(mask, (first < second).astype(jnp.float32), 0).astype(jnp.int32)
    slot = jnp.where(mask > 0.5, rank, -1)
    order = jnp.zeros((count, count), jnp.int32)
    for place in range(SLOTS):
        tile = jnp.sum(jnp.where(slot == place, second, 0), axis=1, keepdims=True)
        order = jnp.where(second == place, tile, order)
    ones = jnp.sum((slot >= 0).astype(jnp.int32), axis=1, keepdims=True)
    order = jnp.where(second == SLOTS, ones, order)
    table_ref[:, :count] = slot
    table_ref[:, count:] = order


def tables(pattern, tile_perm):
    count = pattern.shape[0]
    shape = jax.ShapeDtypeStruct((count, 2 * count), jnp.int32)
    return call(table_kernel, shape, (pattern, tile_perm[:, None]), tables=0)


def place_of(row):
    return row // 4, (row // 2) % 2, row % 2


def pack_kernel(table_ref, strips_ref, packed_ref):
    count = table_ref.shape[0]
    row = lax.axis_index("row")
    per_col = strips_ref.shape[2] // TILE
    ones = table_ref[row, count + SLOTS]
    for place in range(SLOTS):
        tile = table_ref[row, count + place]
        start = pl.multiple_of((tile % per_col) * TILE, TILE)
        block = strips_ref[tile // per_col, :, pl.ds(start, TILE)]
        packed_ref[:, place * TILE : (place + 1) * TILE] = jnp.where(
            place < ones, block, jnp.zeros_like(block)
        )


def pack(table, strips):
    shape = jax.ShapeDtypeStruct((strips.shape[1], SLOTS * TILE), strips.dtype)
    return call(pack_kernel, shape, (table, strips), limit=8)


def fill(table_ref, factor_ref, blocks, places):
    count = table_ref.shape[0]
    depth = factor_ref.shape[0] // SLOTS
    row = lax.axis_index("row")
    z, y_hi, core = place_of(row)
    ones = table_ref[row, count + SLOTS]
    for block, (step, y_flip, core_flip) in zip(blocks, places):
        passed_by = core ^ core_flip
        z_of = (z + Z + step * (2 * passed_by - 1)) % Z
        for half in range(block.shape[0] // depth):
            other = (z_of * Y_HI + (y_hi ^ y_flip)) * CORE + (passed_by ^ half)
            place = table_ref[row, other]

            @pl.when(place >= 0)
            def _(block=block, half=half, other=other, place=place):
                start = pl.multiple_of(place * depth, depth)

                def copy(inner, _):
                    slot = table_ref[other, table_ref[row, count + inner]]

                    @pl.when(slot >= 0)
                    def _():
                        factor_ref[
                            pl.ds(start, depth), pl.ds(pl.multiple_of(inner * TILE, TILE), TILE)
                        ] = block[
                            half * depth : (half + 1) * depth,
                            pl.ds(pl.multiple_of(slot * TILE, TILE), TILE),
                        ]

                    return 0

                lax.fori_loop(0, ones, copy, 0)


def first_kernel(table_ref, *refs, places):
    refs[-1][...] = jnp.zeros_like(refs[-1])
    fill(table_ref, refs[-1], refs[:-1], places)


def next_kernel(table_ref, _, *refs, places):
    fill(table_ref, refs[-1], refs[:-1], places)


def grow(table, factor, arrived, depth):
    blocks, places = zip(*arrived)
    width = blocks[0].shape[1]
    shape = jax.ShapeDtypeStruct((SLOTS * depth, width), blocks[0].dtype)
    if factor is None:
        kernel = functools.partial(first_kernel, places=places)
        return call(kernel, shape, (table, *blocks), limit=8)
    kernel = functools.partial(next_kernel, places=places)
    return call(kernel, shape, (table, factor, *blocks), limit=8, input_output_aliases={1: 0})


def join_kernel(own_ref, far_own_ref, other_ref, far_other_ref, band_ref):
    depth = own_ref.shape[0] // 2
    col = lax.axis_index("col")
    y_lo, x = col // X, col % X
    step = 1 - 2 * place_of(lax.axis_index("row"))[2]
    for ref, y_of, x_steps in (
        (own_ref, y_lo, (0, -step)),
        (far_own_ref, y_lo, (step, 2)),
        (other_ref, 1 - y_lo, (0, -step)),
        (far_other_ref, 1 - y_lo, (step, 2)),
    ):
        for index, x_step in enumerate(x_steps):
            strip = y_of * X + (x + X + x_step) % X
            band_ref[pl.ds(pl.multiple_of(strip * depth, depth), depth), :] = ref[
                index * depth : (index + 1) * depth, :
            ]


def join(*pieces):
    rows, width = pieces[0].shape
    shape = jax.ShapeDtypeStruct((4 * rows, width), pieces[0].dtype)
    return call(join_kernel, shape, pieces, tables=0, limit=8)


MARKS = 16


def code(strips):
    steps, marks = [], []
    for values in strips:
        largest = jnp.max(jnp.abs(values), axis=0, keepdims=True)
        exponent = jnp.floor(jnp.log2(jnp.maximum(largest, 2.0**-100)))
        scaled = jnp.round(values * jnp.exp2(14.0 - exponent))
        steps.append(jnp.clip(scaled, -32767.0, 32767.0))
        marks.append(exponent)
    marks += [jnp.zeros_like(marks[0])] * (MARKS - len(marks))
    return jnp.concatenate(steps, axis=0), jnp.concatenate(marks, axis=0)


def to_16_bits(values):
    return values.astype(jnp.int32).astype(jnp.int16)


def steps_of(coded_ref, strip):
    first = coded_ref.shape[1] - MARKS
    marks = coded_ref[strip, first:, :].astype(jnp.int32).astype(jnp.float32)
    return jnp.exp2(marks - 14.0)


def decode(steps, step):
    return steps.astype(jnp.int32).astype(jnp.float32) * step


def square_kernel(table_ref, _, band_ref, *refs, places):
    blocks, (spread_ref, factor_ref) = refs[:-2], refs[-2:]
    fill(table_ref, factor_ref, blocks, places)
    square = lax.dot_general(
        factor_ref[...],
        band_ref[...],
        (((1,), (1,)), ((), ())),
        preferred_element_type=jnp.float32,
    )
    depth = square.shape[0] // SLOTS
    coded = code([square[place * depth : (place + 1) * depth] for place in range(SLOTS)])
    coded = to_16_bits(jnp.concatenate(coded, axis=0))
    for col in range(COL):
        spread_ref[col] = coded


def square_strips(table, factor, band, arrived):
    blocks, places = zip(*arrived)
    shapes = (
        jax.ShapeDtypeStruct((COL, factor.shape[0] + MARKS, TILE), jnp.int16),
        jax.ShapeDtypeStruct(factor.shape, factor.dtype),
    )
    return call(
        functools.partial(square_kernel, places=places),
        shapes,
        (table, factor, band, *blocks),
        input_output_aliases={1: 1},
    )


def cube_kernel(table_ref, factor_ref, got_ref, coded_ref, held, held_marks, *, scale):
    count = table_ref.shape[0]
    row = lax.axis_index("row")
    cols, rows, _ = got_ref.shape
    depth = (rows - MARKS) // SLOTS
    sizes = [steps_of(got_ref, strip) for strip in range(cols)]
    total = jnp.zeros((SLOTS * depth, got_ref.shape[2]), jnp.float32)
    for place in range(SLOTS):
        tile = []
        for strip in range(cols):
            steps = got_ref[strip, place * depth : (place + 1) * depth, :]
            square = decode(steps, sizes[strip][place : place + 1])
            tile.append(square.astype(jnp.bfloat16))
        total += jnp.dot(
            factor_ref[:, place * TILE : (place + 1) * TILE],
            jnp.concatenate(tile, axis=0),
            preferred_element_type=jnp.float32,
        )
    total *= scale
    steps, marks = code([total[place * depth : (place + 1) * depth] for place in range(SLOTS)])
    held[...] = to_16_bits(steps)
    held_marks[...] = marks
    per_col = count // cols
    for to in range(cols):
        marks = []
        for spot in range(per_col):
            place = table_ref[row, to * per_col + spot]
            first = jnp.maximum(place, 0)
            block = held[pl.ds(pl.multiple_of(first * depth, depth), depth), :]
            coded_ref[to, spot * depth : (spot + 1) * depth, :] = jnp.where(
                place >= 0, block, jnp.zeros_like(block)
            )
            marks.append(held_marks[pl.ds(first, 1), :])
        marks += [jnp.zeros_like(marks[0])] * (MARKS - per_col)
        coded_ref[to, per_col * depth :, :] = to_16_bits(jnp.concatenate(marks, axis=0))


def cube_strips(table, factor, got, scale):
    cols, rows, _ = got.shape
    depth = (rows - MARKS) // SLOTS
    per_col = table.shape[0] // cols
    shape = jax.ShapeDtypeStruct((cols, per_col * depth + MARKS, TILE), jnp.int16)
    return call(
        functools.partial(cube_kernel, scale=scale),
        shape,
        (table, factor, got),
        scratch_shapes=[
            pltpu.VMEM((SLOTS * depth, TILE), jnp.int16),
            pltpu.VMEM((MARKS, TILE), jnp.float32),
        ],
    )


def square_home_kernel(table_ref, got_ref, square_ref, held):
    row, col = lax.axis_index("row"), lax.axis_index("col")
    cols, rows, _ = got_ref.shape
    depth = (rows - MARKS) // SLOTS
    per_col = square_ref.shape[1] // TILE
    sizes = [steps_of(got_ref, strip) for strip in range(cols)]
    index = lax.broadcasted_iota(jnp.int32, sizes[0].shape, 0)
    for spot in range(per_col):
        place = table_ref[row, col * per_col + spot]
        start = pl.multiple_of(jnp.maximum(place, 0) * depth, depth)
        for strip in range(cols):
            size = jnp.sum(jnp.where(index == place, sizes[strip], 0.0), axis=0, keepdims=True)
            held[strip * depth : (strip + 1) * depth, :] = decode(
                got_ref[strip, pl.ds(start, depth), :], size
            )
        square_ref[:, spot * TILE : (spot + 1) * TILE] = held[...].T


def cube_home_kernel(got_ref, cubed_ref, held):
    cols = got_ref.shape[0]
    depth = TILE // cols
    sizes = [steps_of(got_ref, strip) for strip in range(cols)]
    for spot in range(cubed_ref.shape[1] // TILE):
        for strip in range(cols):
            steps = got_ref[strip, spot * depth : (spot + 1) * depth, :]
            held[strip * depth : (strip + 1) * depth, :] = decode(
                steps, sizes[strip][spot : spot + 1]
            )
        cubed_ref[:, spot * TILE : (spot + 1) * TILE] = held[...].T


def home(kernel, operands, tables, shape):
    out = jax.ShapeDtypeStruct(shape, jnp.float32)
    scratch = [pltpu.VMEM((TILE, TILE), jnp.float32)]
    return call(kernel, out, operands, tables=tables, scratch_shapes=scratch)


def local(density, pattern, tile_perm):
    rows, columns = density.shape
    depth = rows // COL
    table = tables(pattern, tile_perm)
    strips = lax.all_to_all(density.reshape(COL, depth, columns), "col", 0, 0)
    packed = pack(table, strips)
    across = to_other_y(packed)
    near = [jnp.concatenate([packed, to_other_core(packed)], 0)]
    far = [jnp.concatenate([across, to_other_core(across)], 0)]

    far.append(along_z(far[0]))
    near.append(along_z(near[0]))
    next_x = along_x(near[0])
    own = jnp.concatenate([packed, next_x[:depth]], 0)
    other = to_other_y_lo(own)
    far_own = jnp.concatenate([to_other_core(next_x[depth:]), along_x(next_x[:depth])], 0)
    far_other = to_other_y_lo(far_own)
    far.append(along_z(far[1]))
    near.append(along_z(near[1]))
    near_swapped, far_swapped = [None], [None]

    def swap(block, swapped, hold):
        hold, arrived = lax.optimization_barrier((hold, to_other_core(block)))
        swapped.append(arrived)
        return hold

    near[2] = swap(near[1], near_swapped, near[2])
    near.append(along_z(near[2]))
    far[2] = swap(far[1], far_swapped, far[2])
    far[2], other = lax.optimization_barrier((far[2], other))
    far.append(along_z(far[2]))
    near[3] = swap(near[2], near_swapped, near[3])

    def both(step, y_flip):
        direct, swapped = (far, far_swapped) if y_flip else (near, near_swapped)
        return [(direct[step], (step, y_flip, 0)), (swapped[step], (step, y_flip, 1))]

    factor = grow(table, None, [(near[0], (0, 0, 0)), (far[0], (0, 1, 0))] + both(1, 0), depth)
    near[3], factor = lax.optimization_barrier((near[3], factor))
    near.append(along_z(near[3][:depth]))
    far_swapped.append(to_other_core(far[2]))
    far.append(along_z(far[3][:depth]))
    for step in (3, 4):
        near_swapped.append(to_other_core(near[step]))
    far_swapped.append(to_other_core(far[3]))
    factor = grow(table, factor, both(1, 1) + both(2, 0) + both(2, 1) + both(3, 0), depth)
    band = join(own, far_own, other, far_other)
    far[4], factor, band = lax.optimization_barrier((far[4], factor, band))
    far_swapped.append(to_other_core(far[4]))
    spread, factor = square_strips(
        table, factor, band, both(3, 1) + both(4, 0) + both(4, 1)
    )
    got = lax.all_to_all(spread, "col", 0, 0)
    scale = (rows * lax.axis_size("row") / 2.0) ** (-0.25)
    coded = cube_strips(table, factor, got, scale)
    square = home(square_home_kernel, (table, got), 1, (rows, columns))
    cubed = home(cube_home_kernel, (lax.all_to_all(coded, "col", 0, 0),), 0, (rows, columns))
    return square, cubed


def solution(mesh):
    return jax.shard_map(
        local,
        mesh=mesh,
        in_specs=(P("row", "col"), P(), P()),
        out_specs=(P("row", "col"), P("row", "col")),
        check_vma=False,
    )
```

```python
import functools

import jax
import jax.numpy as jnp
from jax import lax
from jax.experimental import pallas as pl
from jax.experimental.pallas import tpu as pltpu
from jax.sharding import PartitionSpec as P

TILE = 256
SLOTS = 13
BOTH = ("row", "col")
MIB = 1024 * 1024
VMEM = pl.BlockSpec(memory_space=pltpu.VMEM)
SMEM = pl.BlockSpec(memory_space=pltpu.SMEM)

Z, Y_HI, CORE, COL, X = 8, 2, 2, 8, 4


def device(z, y_hi, core, col):
    return ((z % Z * Y_HI + y_hi % Y_HI) * CORE + core % CORE) * COL + col


def pairs(move):
    places = [
        (z, y_hi, core, col)
        for z in range(Z)
        for y_hi in range(Y_HI)
        for core in range(CORE)
        for col in range(COL)
    ]
    return [(device(*place), device(*move(*place))) for place in places]


def move(block, place):
    return lax.ppermute(block, BOTH, pairs(place))


def to_other_core(block):
    return move(block, lambda z, y, core, col: (z, y, core + 1, col))


def to_other_y(block):
    return move(block, lambda z, y, core, col: (z, y + 1, core, col))


def to_other_y_lo(block):
    return move(block, lambda z, y, core, col: (z, y, core, (col + X) % COL))


def along_x(block):
    return move(
        block,
        lambda z, y, core, col: (z, y, core, col // X * X + (col + 1 - 2 * core) % X),
    )


def along_z(block, steps=1):
    return move(block, lambda z, y, core, col: (z + steps * (1 - 2 * core), y, core, col))


def call(kernel, out_shape, operands, tables=1, limit=16, **options):
    return pl.pallas_call(
        kernel,
        out_shape=out_shape,
        in_specs=[SMEM] * tables + [VMEM] * (len(operands) - tables),
        out_specs=jax.tree.map(lambda _: VMEM, out_shape),
        compiler_params=pltpu.CompilerParams(vmem_limit_bytes=limit * MIB),
        **options,
    )(*operands)


def table_kernel(pattern_ref, perm_ref, table_ref):
    count = pattern_ref.shape[0]
    first = lax.broadcasted_iota(jnp.int32, (count, count), 0)
    second = lax.broadcasted_iota(jnp.int32, (count, count), 1)
    pattern = pattern_ref[...].astype(jnp.float32)
    one_hot = (perm_ref[...] == second).astype(jnp.float32)
    upper = jnp.where(first <= second, pattern, 0.0)
    strict = jnp.where(first < second, pattern, 0.0)

    def dot(a, b, b_dim):
        return lax.dot_general(
            a, b, (((1,), (b_dim,)), ((), ())), preferred_element_type=jnp.float32
        )

    mask = dot(dot(one_hot, upper, 0) + dot(one_hot, strict, 1), one_hot, 1)
    rank = dot(mask, (first < second).astype(jnp.float32), 0).astype(jnp.int32)
    slot = jnp.where(mask > 0.5, rank, -1)
    order = jnp.zeros((count, count), jnp.int32)
    for place in range(SLOTS):
        tile = jnp.sum(jnp.where(slot == place, second, 0), axis=1, keepdims=True)
        order = jnp.where(second == place, tile, order)
    ones = jnp.sum((slot >= 0).astype(jnp.int32), axis=1, keepdims=True)
    order = jnp.where(second == SLOTS, ones, order)
    table_ref[:, :count] = slot
    table_ref[:, count:] = order


def tables(pattern, tile_perm):
    count = pattern.shape[0]
    shape = jax.ShapeDtypeStruct((count, 2 * count), jnp.int32)
    return call(table_kernel, shape, (pattern, tile_perm[:, None]), tables=0)


def place_of(row):
    return row // 4, (row // 2) % 2, row % 2


def pack_kernel(table_ref, strips_ref, packed_ref):
    count = table_ref.shape[0]
    row = lax.axis_index("row")
    per_col = strips_ref.shape[2] // TILE
    ones = table_ref[row, count + SLOTS]
    for place in range(SLOTS):
        tile = table_ref[row, count + place]
        start = pl.multiple_of((tile % per_col) * TILE, TILE)
        block = strips_ref[tile // per_col, :, pl.ds(start, TILE)]
        packed_ref[:, place * TILE : (place + 1) * TILE] = jnp.where(
            place < ones, block, jnp.zeros_like(block)
        )


def pack(table, strips):
    shape = jax.ShapeDtypeStruct((strips.shape[1], SLOTS * TILE), strips.dtype)
    return call(pack_kernel, shape, (table, strips), limit=8)


def fill(table_ref, factor_ref, blocks, places):
    count = table_ref.shape[0]
    depth = factor_ref.shape[0] // SLOTS
    row = lax.axis_index("row")
    z, y_hi, core = place_of(row)
    ones = table_ref[row, count + SLOTS]
    for block, (step, y_flip, core_flip) in zip(blocks, places):
        passed_by = core ^ core_flip
        z_of = (z + Z + step * (2 * passed_by - 1)) % Z
        for half in range(block.shape[0] // depth):
            other = (z_of * Y_HI + (y_hi ^ y_flip)) * CORE + (passed_by ^ half)
            place = table_ref[row, other]

            @pl.when(place >= 0)
            def _(block=block, half=half, other=other, place=place):
                start = pl.multiple_of(place * depth, depth)

                def copy(inner, _):
                    slot = table_ref[other, table_ref[row, count + inner]]

                    @pl.when(slot >= 0)
                    def _():
                        factor_ref[
                            pl.ds(start, depth), pl.ds(pl.multiple_of(inner * TILE, TILE), TILE)
                        ] = block[
                            half * depth : (half + 1) * depth,
                            pl.ds(pl.multiple_of(slot * TILE, TILE), TILE),
                        ]

                    return 0

                lax.fori_loop(0, ones, copy, 0)


def first_kernel(table_ref, *refs, places):
    refs[-1][...] = jnp.zeros_like(refs[-1])
    fill(table_ref, refs[-1], refs[:-1], places)


def next_kernel(table_ref, _, *refs, places):
    fill(table_ref, refs[-1], refs[:-1], places)


def grow(table, factor, arrived, depth):
    blocks, places = zip(*arrived)
    width = blocks[0].shape[1]
    shape = jax.ShapeDtypeStruct((SLOTS * depth, width), blocks[0].dtype)
    if factor is None:
        kernel = functools.partial(first_kernel, places=places)
        return call(kernel, shape, (table, *blocks), limit=8)
    kernel = functools.partial(next_kernel, places=places)
    return call(kernel, shape, (table, factor, *blocks), limit=8, input_output_aliases={1: 0})


def join_kernel(own_ref, far_own_ref, other_ref, far_other_ref, band_ref):
    depth = own_ref.shape[0] // 2
    col = lax.axis_index("col")
    y_lo, x = col // X, col % X
    step = 1 - 2 * place_of(lax.axis_index("row"))[2]
    for ref, y_of, x_steps in (
        (own_ref, y_lo, (0, -step)),
        (far_own_ref, y_lo, (step, 2)),
        (other_ref, 1 - y_lo, (0, -step)),
        (far_other_ref, 1 - y_lo, (step, 2)),
    ):
        for index, x_step in enumerate(x_steps):
            strip = y_of * X + (x + X + x_step) % X
            band_ref[pl.ds(pl.multiple_of(strip * depth, depth), depth), :] = ref[
                index * depth : (index + 1) * depth, :
            ]


def join(*pieces):
    rows, width = pieces[0].shape
    shape = jax.ShapeDtypeStruct((4 * rows, width), pieces[0].dtype)
    return call(join_kernel, shape, pieces, tables=0, limit=8)


MARKS = 16


def code(strips):
    steps, marks = [], []
    for values in strips:
        largest = jnp.max(jnp.abs(values), axis=0, keepdims=True)
        exponent = jnp.floor(jnp.log2(jnp.maximum(largest, 2.0**-100)))
        scaled = jnp.round(values * jnp.exp2(14.0 - exponent))
        steps.append(jnp.clip(scaled, -32767.0, 32767.0))
        marks.append(exponent)
    marks += [jnp.zeros_like(marks[0])] * (MARKS - len(marks))
    return jnp.concatenate(steps, axis=0), jnp.concatenate(marks, axis=0)


def to_16_bits(values):
    return values.astype(jnp.int32).astype(jnp.int16)


def steps_of(coded_ref, strip):
    first = coded_ref.shape[1] - MARKS
    marks = coded_ref[strip, first:, :].astype(jnp.int32).astype(jnp.float32)
    return jnp.exp2(marks - 14.0)


def decode(steps, step):
    return steps.astype(jnp.int32).astype(jnp.float32) * step


def square_kernel(table_ref, _, band_ref, *refs, places):
    blocks, (spread_ref, factor_ref) = refs[:-2], refs[-2:]
    fill(table_ref, factor_ref, blocks, places)
    square = lax.dot_general(
        factor_ref[...],
        band_ref[...],
        (((1,), (1,)), ((), ())),
        preferred_element_type=jnp.float32,
    )
    depth = square.shape[0] // SLOTS
    coded = code([square[place * depth : (place + 1) * depth] for place in range(SLOTS)])
    coded = to_16_bits(jnp.concatenate(coded, axis=0))
    for col in range(COL):
        spread_ref[col] = coded


def square_strips(table, factor, band, arrived):
    blocks, places = zip(*arrived)
    shapes = (
        jax.ShapeDtypeStruct((COL, factor.shape[0] + MARKS, TILE), jnp.int16),
        jax.ShapeDtypeStruct(factor.shape, factor.dtype),
    )
    return call(
        functools.partial(square_kernel, places=places),
        shapes,
        (table, factor, band, *blocks),
        input_output_aliases={1: 1},
    )


def cube_kernel(table_ref, factor_ref, got_ref, coded_ref, held, held_marks, *, scale):
    count = table_ref.shape[0]
    row = lax.axis_index("row")
    cols, rows, _ = got_ref.shape
    depth = (rows - MARKS) // SLOTS
    sizes = [steps_of(got_ref, strip) for strip in range(cols)]
    total = jnp.zeros((SLOTS * depth, got_ref.shape[2]), jnp.float32)
    for place in range(SLOTS):
        tile = []
        for strip in range(cols):
            steps = got_ref[strip, place * depth : (place + 1) * depth, :]
            square = decode(steps, sizes[strip][place : place + 1])
            tile.append(square.astype(jnp.bfloat16))
        total += jnp.dot(
            factor_ref[:, place * TILE : (place + 1) * TILE],
            jnp.concatenate(tile, axis=0),
            preferred_element_type=jnp.float32,
        )
    total *= scale
    steps, marks = code([total[place * depth : (place + 1) * depth] for place in range(SLOTS)])
    held[...] = to_16_bits(steps)
    held_marks[...] = marks
    per_col = count // cols
    for to in range(cols):
        marks = []
        for spot in range(per_col):
            place = table_ref[row, to * per_col + spot]
            first = jnp.maximum(place, 0)
            block = held[pl.ds(pl.multiple_of(first * depth, depth), depth), :]
            coded_ref[to, spot * depth : (spot + 1) * depth, :] = jnp.where(
                place >= 0, block, jnp.zeros_like(block)
            )
            marks.append(held_marks[pl.ds(first, 1), :])
        marks += [jnp.zeros_like(marks[0])] * (MARKS - per_col)
        coded_ref[to, per_col * depth :, :] = to_16_bits(jnp.concatenate(marks, axis=0))


def cube_strips(table, factor, got, scale):
    cols, rows, _ = got.shape
    depth = (rows - MARKS) // SLOTS
    per_col = table.shape[0] // cols
    shape = jax.ShapeDtypeStruct((cols, per_col * depth + MARKS, TILE), jnp.int16)
    return call(
        functools.partial(cube_kernel, scale=scale),
        shape,
        (table, factor, got),
        scratch_shapes=[
            pltpu.VMEM((SLOTS * depth, TILE), jnp.int16),
            pltpu.VMEM((MARKS, TILE), jnp.float32),
        ],
    )


def square_home_kernel(table_ref, got_ref, square_ref, held):
    row, col = lax.axis_index("row"), lax.axis_index("col")
    cols, rows, _ = got_ref.shape
    depth = (rows - MARKS) // SLOTS
    per_col = square_ref.shape[1] // TILE
    sizes = [steps_of(got_ref, strip) for strip in range(cols)]
    index = lax.broadcasted_iota(jnp.int32, sizes[0].shape, 0)
    for spot in range(per_col):
        place = table_ref[row, col * per_col + spot]
        start = pl.multiple_of(jnp.maximum(place, 0) * depth, depth)
        for strip in range(cols):
            size = jnp.sum(jnp.where(index == place, sizes[strip], 0.0), axis=0, keepdims=True)
            held[strip * depth : (strip + 1) * depth, :] = decode(
                got_ref[strip, pl.ds(start, depth), :], size
            )
        square_ref[:, spot * TILE : (spot + 1) * TILE] = held[...].T


def cube_home_kernel(got_ref, cubed_ref, held):
    spot = pl.program_id(0)
    cols = got_ref.shape[0]
    depth = TILE // cols
    start = pl.multiple_of(spot * depth, depth)
    for strip in range(cols):
        sizes = steps_of(got_ref, strip)
        index = lax.broadcasted_iota(jnp.int32, sizes.shape, 0)
        size = jnp.sum(jnp.where(index == spot, sizes, 0.0), axis=0, keepdims=True)
        held[strip * depth : (strip + 1) * depth, :] = decode(
            got_ref[strip, pl.ds(start, depth), :], size
        )
    cubed_ref[...] = held[...].T


def cube_home(got, shape):
    return pl.pallas_call(
        cube_home_kernel,
        grid=(shape[1] // TILE,),
        out_shape=jax.ShapeDtypeStruct(shape, jnp.float32),
        in_specs=[pl.BlockSpec(got.shape, lambda spot: (0, 0, 0))],
        out_specs=pl.BlockSpec((shape[0], TILE), lambda spot: (0, spot)),
        scratch_shapes=[pltpu.VMEM((TILE, TILE), jnp.float32)],
        compiler_params=pltpu.CompilerParams(vmem_limit_bytes=16 * MIB),
    )(got)


def home(kernel, operands, tables, shape):
    out = jax.ShapeDtypeStruct(shape, jnp.float32)
    scratch = [pltpu.VMEM((TILE, TILE), jnp.float32)]
    return call(kernel, out, operands, tables=tables, scratch_shapes=scratch)


def local(density, pattern, tile_perm):
    rows, columns = density.shape
    depth = rows // COL
    table = tables(pattern, tile_perm)
    strips = lax.all_to_all(density.reshape(COL, depth, columns), "col", 0, 0)
    packed = pack(table, strips)
    across = to_other_y(packed)
    near = [jnp.concatenate([packed, to_other_core(packed)], 0)]
    far = [jnp.concatenate([across, to_other_core(across)], 0)]

    far.append(along_z(far[0]))
    near.append(along_z(near[0]))
    next_x = along_x(near[0])
    own = jnp.concatenate([packed, next_x[:depth]], 0)
    other = to_other_y_lo(own)
    far_own = jnp.concatenate([to_other_core(next_x[depth:]), along_x(next_x[:depth])], 0)
    far_other = to_other_y_lo(far_own)
    far.append(along_z(far[1]))
    near.append(along_z(near[1]))
    near_swapped, far_swapped = [None], [None]

    def swap(block, swapped, hold):
        hold, arrived = lax.optimization_barrier((hold, to_other_core(block)))
        swapped.append(arrived)
        return hold

    near[2] = swap(near[1], near_swapped, near[2])
    near.append(along_z(near[2]))
    far[2] = swap(far[1], far_swapped, far[2])
    far[2], other = lax.optimization_barrier((far[2], other))
    far.append(along_z(far[2]))
    near[3] = swap(near[2], near_swapped, near[3])

    def both(step, y_flip):
        direct, swapped = (far, far_swapped) if y_flip else (near, near_swapped)
        return [(direct[step], (step, y_flip, 0)), (swapped[step], (step, y_flip, 1))]

    factor = grow(table, None, [(near[0], (0, 0, 0)), (far[0], (0, 1, 0))] + both(1, 0), depth)
    near[3], factor = lax.optimization_barrier((near[3], factor))
    near.append(along_z(near[3][:depth]))
    far_swapped.append(to_other_core(far[2]))
    far.append(along_z(far[3][:depth]))
    for step in (3, 4):
        near_swapped.append(to_other_core(near[step]))
    far_swapped.append(to_other_core(far[3]))
    factor = grow(table, factor, both(1, 1) + both(2, 0) + both(2, 1) + both(3, 0), depth)
    band = join(own, far_own, other, far_other)
    far[4], factor, band = lax.optimization_barrier((far[4], factor, band))
    far_swapped.append(to_other_core(far[4]))
    spread, factor = square_strips(
        table, factor, band, both(3, 1) + both(4, 0) + both(4, 1)
    )
    got = lax.all_to_all(spread, "col", 0, 0)
    scale = (rows * lax.axis_size("row") / 2.0) ** (-0.25)
    coded = cube_strips(table, factor, got, scale)
    square = home(square_home_kernel, (table, got), 1, (rows, columns))
    cubed = cube_home(lax.all_to_all(coded, "col", 0, 0), (rows, columns))
    return square, cubed


def solution(mesh):
    return jax.shard_map(
        local,
        mesh=mesh,
        in_specs=(P("row", "col"), P(), P()),
        out_specs=(P("row", "col"), P("row", "col")),
        check_vma=False,
    )
```
